32 devices in a mesh: slab: 8 (over z, y), chan: 4 (over x, core).
Axes of the slice: x: 2, y: 2, z: 4, core: 2. Of those that a mesh axis runs over, the one named last changes fastest.
Arguments:
- field: bfloat16 [32, 256, 256, 256], P('chan', 'slab'), may hold values from -6 to 6
- forcing: bfloat16 [256, 256, 256], P('slab', 'chan'), may hold values from -6 to 6
- slot_column: int32 [8, 256], replicated, may hold values from -1 to 1023, as said below
- w_spec: bfloat16 [2, 32, 32, 32768], P(None, 'chan', None, 'slab'), may hold values from -12 to 12
- skip_gain: float32 [32], P('chan'), may hold values from 0.5 to 1.5
- bias: float32 [32], P('chan'), may hold values from -3 to 3
Outputs:
- output: bfloat16 [32, 256, 256, 256], P('chan', 'slab')
- gradient: bfloat16 [32, 256, 256, 256], P('chan', 'slab')
The draws below stay inside these ranges and needn't reach their ends.
Inputs may be any that keep to these rules, and one draw needn't show every extreme that they name: `slot_column`: every kept pair index 0 to 1023 appears exactly once in the table; empty slots hold -1; the busiest slab device fills all 256 of its slots.
All inputs are finite; a program needn't handle non-finite values.
Results may differ from the reference program's by a relative error of at most 0.022.
Values may be sent and summed in bfloat16 or wider, within the bound.
No kernel may reach another device: no remote copies, remote signals or barrier semaphores. Data moves between devices by JAX's collectives and lax.ppermute only.
A program may use at most 256 MiB of HBM per device.

```python
import math
import jax
import jax.numpy as jnp
from jax import lax

GRID = 256
CH = 32
KXY = 32
KZ = 16
CAP = 256
N_SLAB = 8


def draw_slot_column(key, part):
    columns = KXY * KXY
    slabs = 2 * columns // CAP
    average = columns // slabs
    key_delta = jax.random.fold_in(key, 11)
    key_order = jax.random.fold_in(key, 23)
    key_cols = jax.random.fold_in(key, 37)
    deltas = jax.random.randint(key_delta, (slabs // 2,), 0, average // 2 + 1).astype(jnp.int32)
    deltas = deltas.at[0].set(average)
    paired = jnp.stack([average + deltas, average - deltas], axis=1).reshape(slabs)
    order = jax.random.permutation(key_order, slabs)
    counts = jnp.zeros((slabs,), jnp.int32).at[order].set(paired)
    offsets = jnp.cumsum(counts) - counts
    shuffled = jax.random.permutation(key_cols, columns).astype(jnp.int32)
    slot_ids = jnp.arange(CAP, dtype=jnp.int32)
    wanted = offsets[:, None] + slot_ids[None, :]
    occupied = slot_ids[None, :] < counts[:, None]
    picked = shuffled[jnp.clip(wanted, 0, columns - 1)]
    return jnp.where(occupied, picked, -1).astype(jnp.int32)


def shard_levels(stream_key, shape, shards, low, top_value):
    factor_of = 1.0
    for axis_at, shards_of in shards:
        steps = jax.random.uniform(jax.random.fold_in(jax.random.fold_in(stream_key, 6), axis_at), (shards_of,), jnp.float32, low / len(shards), top_value / len(shards))
        factor_of = factor_of * jnp.repeat(jnp.exp(steps), shape[axis_at] // shards_of).reshape((-1,) + (1,) * (len(shape) - 1 - axis_at))
    return factor_of


def noise(rng, dims, deviation, most, split=(), held_as=jnp.bfloat16):
    values = deviation * jax.random.normal(rng, dims, jnp.float32)
    if split:
        values = values * shard_levels(rng, dims, split, -0.22, 0.18)
    return jnp.clip(values, -most, most).astype(held_as)


def setup_inputs(seed: int = 0) -> dict:
    splits = jax.random.split(jax.random.key(seed), 7)
    field = noise(splits[0], (CH, GRID, GRID, GRID), 1.0, 6.0, ((0, 4), (1, 8)))
    forcing = noise(splits[1], (GRID, GRID, GRID), 1.0, 6.0, ((0, 8), (1, 4)))
    slot_column = draw_slot_column(jax.random.fold_in(splits[6], 71), 0)
    w_spec = noise(splits[3], (2, CH, CH, N_SLAB * CAP * KZ), 2.0, 12.0, ((1, 4), (3, 8)))
    skip_gain = jnp.clip(0.5 + 1.0 * jax.random.uniform(splits[4], (CH,), jnp.float32) ** shard_levels(splits[4], (CH,), ((0, 4),), -0.2, 0.2), 0.5, 1.5)
    bias = noise(splits[5], (CH,), 0.5, 3.0, ((0, 4),), jnp.float32)
    return {"field": field, "forcing": forcing, "slot_column": slot_column, "w_spec": w_spec, "skip_gain": skip_gain, "bias": bias}


def angle_pair(freqs, coords, grid_len):
    turns = freqs[:, None] * coords[None, :] % grid_len
    angle = turns.astype(jnp.float32) * (2.0 * math.pi / grid_len)
    return (jnp.cos(angle), jnp.sin(angle))

def plane_tables(kept, grid_len):
    freqs = jnp.arange(kept, dtype=jnp.int32) - kept // 2
    coords = jnp.arange(grid_len, dtype=jnp.int32)
    cosine, sine = angle_pair(freqs, coords, grid_len)
    row_table = jnp.concatenate([cosine.T, -sine.T], axis=1).astype(jnp.bfloat16)
    col_table = jnp.stack([cosine, sine]).astype(jnp.bfloat16)
    return (row_table, col_table)

def depth_table(kept_z, start, count, grid_len):
    freqs = jnp.arange(kept_z, dtype=jnp.int32)
    coords = start + jnp.arange(count, dtype=jnp.int32)
    cosine, sine = angle_pair(freqs, coords, grid_len)
    return jnp.stack([cosine, sine]).astype(jnp.float32)

def slot_positions(slot_column, columns):
    flat_slots = slot_column.reshape(-1)
    slot_ids = jnp.arange(flat_slots.shape[0], dtype=jnp.int32)
    matches = flat_slots[None, :] == jnp.arange(columns, dtype=jnp.int32)[:, None]
    return lax.optimization_barrier(jnp.sum(jnp.where(matches, slot_ids[None, :], 0), axis=1)).astype(jnp.int32)

def gelu_parts(preact):
    coeff = math.sqrt(2.0 / math.pi)
    inner = coeff * (preact + 0.044715 * preact ** 3)
    tangent = jnp.tanh(inner)
    value = 0.5 * preact * (1.0 + tangent)
    slope = 0.5 * (1.0 + tangent) + 0.5 * preact * (1.0 - tangent * tangent) * coeff * (1.0 + 3.0 * 0.044715 * preact * preact)
    return (value, slope)

def reference(field, forcing, slot_column, w_spec, skip_gain, bias):
    grid_len = GRID
    kept = KXY
    columns = KXY * KXY
    factor = grid_len ** (-1.5)
    highest = lax.Precision.HIGHEST
    row_table, col_table = plane_tables(kept, grid_len)
    col_wide = col_table.astype(jnp.float32)
    depth = depth_table(KZ, 0, grid_len, grid_len)
    position = slot_positions(slot_column, columns)

    def analyse(volume):
        rows_done = jnp.dot(volume, row_table, preferred_element_type=jnp.float32).astype(jnp.bfloat16)
        mixed_x = jnp.einsum('tkx,zxj->tkjz', col_wide, rows_done.astype(jnp.float32))
        real_part = mixed_x[0, :, :kept] + mixed_x[1, :, kept:]
        imag_part = mixed_x[0, :, kept:] - mixed_x[1, :, :kept]
        pencils = jnp.stack([real_part, imag_part], 2).reshape(columns, 2, grid_len)
        terms = jnp.einsum('tfz,qrz->trqf', depth, pencils, precision=highest)
        return jnp.stack([terms[0, 0] + terms[1, 1], terms[0, 1] - terms[1, 0]], 1) * factor

    def synthesise(spectra):
        terms = jnp.einsum('tfz,qrf->tqrz', depth, spectra, precision=highest)
        planes = jnp.stack([terms[0, :, 0] - terms[1, :, 1], terms[1, :, 0] + terms[0, :, 1]], 1)
        planes = planes.astype(jnp.bfloat16).reshape(kept, kept, 2, grid_len)
        mixed_x = jnp.einsum('tkx,kjrz->trzxj', col_wide, planes.astype(jnp.float32))
        joined = jnp.concatenate([mixed_x[0, 0] - mixed_x[1, 1], mixed_x[1, 0] + mixed_x[0, 1]], -1).astype(jnp.bfloat16)
        return jnp.dot(joined, row_table.T, preferred_element_type=jnp.float32) * factor

    def merge_one(volume):
        return (volume.astype(jnp.float32) + forcing.astype(jnp.float32)).astype(jnp.bfloat16)
    coeffs = lax.map(lambda volume: analyse(merge_one(volume)), field)
    weights = jnp.take(w_spec.reshape(2, CH, CH, N_SLAB * CAP, KZ), position, axis=3).astype(jnp.float32)
    w_real, w_imag = (weights[0], weights[1])
    doubling = jnp.where(jnp.arange(KZ) == 0, 1.0, 2.0).astype(jnp.float32)
    u_real, u_imag = (coeffs[:, :, 0], coeffs[:, :, 1])
    out_real = jnp.einsum('cokf,ckf->okf', w_real, u_real, precision=highest) - jnp.einsum('cokf,ckf->okf', w_imag, u_imag, precision=highest)
    out_imag = jnp.einsum('cokf,ckf->okf', w_imag, u_real, precision=highest) + jnp.einsum('cokf,ckf->okf', w_real, u_imag, precision=highest)
    mixed = jnp.stack([out_real, out_imag], 2) * doubling

    def forward_one(items):
        volume, spectra, gain, shift = items
        merged = merge_one(volume)
        preact = synthesise(spectra) + gain * merged.astype(jnp.float32) + shift
        value, slope = gelu_parts(preact)
        output = value.astype(jnp.bfloat16)
        return (output, output.astype(jnp.float32) * slope)
    output, grad_pre = lax.map(forward_one, (field, mixed, skip_gain, bias))
    back = lax.map(lambda volume: analyse(volume.astype(jnp.bfloat16)), grad_pre) * doubling
    g_real, g_imag = (back[:, :, 0], back[:, :, 1])
    adj_real = jnp.einsum('cokf,okf->ckf', w_real, g_real, precision=highest) + jnp.einsum('cokf,okf->ckf', w_imag, g_imag, precision=highest)
    adj_imag = jnp.einsum('cokf,okf->ckf', w_real, g_imag, precision=highest) - jnp.einsum('cokf,okf->ckf', w_imag, g_real, precision=highest)
    adjoint = jnp.stack([adj_real, adj_imag], 2)

    def backward_one(items):
        spectra, grad_one, gain = items
        return (synthesise(spectra) + gain * grad_one).astype(jnp.bfloat16)
    gradient = lax.map(backward_one, (adjoint, grad_pre, skip_gain))
    return (output, gradient)
```

```python
import functools
import math

import jax
import jax.numpy as jnp
import ml_dtypes
import numpy as np
from jax import lax
from jax.experimental import pallas as pl
from jax.experimental.pallas import tpu as pltpu
from jax.sharding import PartitionSpec as P

KXY = 32
KZ = 16
ZB = 4
HALF = ZB * KXY
C1 = math.sqrt(2.0 / math.pi)
C2 = 0.044715
F32 = jnp.float32
BF16 = jnp.bfloat16
SLOTS = 128
VMEM = 56 * 2**20


def dot(a, b):
    return jnp.dot(a, b, preferred_element_type=F32)


def angles(freqs, count, grid_len):
    turns = (freqs[:, None] * np.arange(count)[None, :]) % grid_len
    return turns * (2.0 * math.pi / grid_len)


def half_width(table):
    return table.astype(ml_dtypes.bfloat16)


def plane_tables(grid_len):
    angle = angles(np.arange(KXY) - KXY // 2, grid_len, grid_len)
    cosine, sine = np.cos(angle), np.sin(angle)
    rows = np.zeros((ZB, grid_len, 2, ZB, KXY))
    for i in range(ZB):
        rows[i, :, 0, i, :] = cosine.T
        rows[i, :, 1, i, :] = -sine.T
    rows = rows.reshape(ZB, grid_len, 2 * HALF)
    return rows, np.concatenate([cosine, sine], 0)


def depth_tables(planes, grid_len):
    angle = angles(np.arange(KZ), planes, grid_len)
    cosine, sine = np.cos(angle), np.sin(angle)
    table = np.zeros((planes // ZB, 2, ZB, KXY, 2, KZ, KXY))
    for b in range(planes // ZB):
        for i in range(ZB):
            for j in range(KXY):
                table[b, 0, i, j, 0, :, j] = cosine[:, b * ZB + i]
                table[b, 1, i, j, 0, :, j] = sine[:, b * ZB + i]
                table[b, 0, i, j, 1, :, j] = -sine[:, b * ZB + i]
                table[b, 1, i, j, 1, :, j] = cosine[:, b * ZB + i]
    return table.reshape(planes // ZB, 2 * HALF, 2 * KZ * KXY)


def spread_table():
    return np.repeat(np.eye(SLOTS), KZ, axis=1)


def whole(array):
    return pl.BlockSpec(array.shape, lambda *_: (0,) * len(array.shape))


def scalars():
    return pl.BlockSpec(memory_space=pltpu.SMEM)


def column_sums(u_ref, rt_ref, p_ref, channels):
    total = dot(u_ref[0], rt_ref[0])
    for i in range(1, ZB):
        total += dot(u_ref[i], rt_ref[i])
    total = total.reshape(channels, 2 * KXY, 2 * HALF)
    low, high = total[:, :KXY], total[:, KXY:]
    real = low[:, :, :HALF] + high[:, :, HALF:]
    imag = low[:, :, HALF:] - high[:, :, :HALF]
    p_ref[:, :HALF] = real.reshape(channels * KXY, HALF).astype(BF16)
    p_ref[:, HALF:] = imag.reshape(channels * KXY, HALF).astype(BF16)


def add_depth(p_ref, tz_ref, ph_ref, acc_ref, out_ref, factor):
    step = pl.program_id(0)
    new = dot(p_ref[...], tz_ref[0])

    @pl.when(step == 0)
    def _():
        acc_ref[...] = new

    @pl.when(step > 0)
    def _():
        acc_ref[...] += new

    @pl.when(step == pl.num_programs(0) - 1)
    def _():
        half = KZ * KXY
        cosine, sine = ph_ref[0:1, :], ph_ref[1:2, :]
        real, imag = acc_ref[:, :half], acc_ref[:, half:]
        out_ref[:, :half] = ((real * cosine + imag * sine) * factor).astype(BF16)
        out_ref[:, half:] = ((imag * cosine - real * sine) * factor).astype(BF16)


def turn_spectra(q_ref, ph_ref, turned_ref):
    @pl.when(pl.program_id(0) == 0)
    def _():
        half = KZ * KXY
        cosine, sine = ph_ref[0:1, :], ph_ref[1:2, :]
        real, imag = q_ref[:, :half].astype(F32), q_ref[:, half:].astype(F32)
        turned_ref[:, :half] = (real * cosine - imag * sine).astype(BF16)
        turned_ref[:, half:] = (real * sine + imag * cosine).astype(BF16)


def column_fields(zz_ref, txt, c):
    row = pl.multiple_of(c * KXY, KXY)
    low = zz_ref[pl.ds(row, KXY), :]
    high = jnp.concatenate([-low[:, HALF:], low[:, :HALF]], 1)
    return dot(txt, jnp.concatenate([low, high], 0)).astype(BF16)


def plane_rows(u_ref, tx, c, i, plane):
    row = pl.multiple_of(c * 2 * KXY, 2 * KXY)
    u_ref[i, pl.ds(row, 2 * KXY), :] = dot(tx, plane).astype(BF16)


def analyse_kernel(channels, factor, v_ref, rt_ref, tx_ref, tz_ref, ph_ref, out_ref, acc_ref, p_ref, u_ref):
    tx = tx_ref[...]

    def body(c, carry):
        for i in range(ZB):
            plane_rows(u_ref, tx, c, i, v_ref[c, i])
        return carry

    lax.fori_loop(0, channels, body, 0, unroll=min(channels, 4))
    column_sums(u_ref, rt_ref, p_ref, channels)
    add_depth(p_ref, tz_ref, ph_ref, acc_ref, out_ref, factor)


def analyse(volume, rt, tx, tz, phase, factor):
    channels, planes, rows, grid_len = volume.shape
    width = 2 * KZ * KXY
    return pl.pallas_call(
        functools.partial(analyse_kernel, channels, factor),
        grid=(planes // ZB,),
        in_specs=[
            pl.BlockSpec((channels, ZB, rows, grid_len), lambda b: (0, b, 0, 0)),
            whole(rt),
            whole(tx),
            pl.BlockSpec((1,) + tz.shape[1:], lambda b: (b, 0, 0)),
            whole(phase),
        ],
        out_specs=pl.BlockSpec((channels * KXY, width), lambda b: (0, 0)),
        out_shape=jax.ShapeDtypeStruct((channels * KXY, width), BF16),
        scratch_shapes=[
            pltpu.VMEM((channels * KXY, width), F32),
            pltpu.VMEM((channels * KXY, 2 * HALF), BF16),
            pltpu.VMEM((ZB, channels * 2 * KXY, grid_len), BF16),
        ],
        compiler_params=pltpu.CompilerParams(vmem_limit_bytes=VMEM),
        cost_estimate=pl.CostEstimate(
            flops=512 * volume.size, bytes_accessed=2 * volume.size, transcendentals=0
        ),
        name="analyse",
    )(volume, rt, tx, tz, phase)


def gelu_planes(field, coefs_ref, c):
    cubic, linear, half, square = (coefs_ref[c, k].astype(BF16) for k in range(4))
    squared = field * field
    inner = field * (squared * cubic + linear)
    tangent = jnp.tanh(inner.astype(F32))
    upper = (1.0 + tangent).astype(BF16)
    lower = (1.0 - tangent).astype(BF16)
    value = field * (upper * half)
    slope = upper + value * lower * (squared * square + BF16(2.0 * C1))
    return value, value * slope


def middle_kernel(
    channels, factor, q_ref, v_ref, f_ref, coefs_ref, scale_ref, shift_ref, rt_ref, bd_ref, tx_ref, txt_ref,
    tz_ref, ts_ref, ph_ref, o_ref, g_ref, back_ref, acc_ref, p_ref, u_ref, zz_ref, turned_ref, x_ref,
):
    turn_spectra(q_ref, ph_ref, turned_ref)
    zz_ref[...] = (dot(turned_ref[...], ts_ref[0]) * scale_ref[...] + shift_ref[...]).astype(BF16)
    tx, txt = tx_ref[...], txt_ref[...]

    def columns(c, carry):
        x_ref[c] = column_fields(zz_ref, txt, c)
        return carry

    lax.fori_loop(0, channels, columns, 0, unroll=min(channels, 4))

    def forward(c):
        for i in range(ZB):
            spatial = dot(x_ref[c], bd_ref[i]).astype(BF16)
            value, grad = gelu_planes(spatial + (v_ref[c, i] + f_ref[i]), coefs_ref, c)
            o_ref[c, i] = value
            g_ref[c, i] = grad

    def backward(c):
        for i in range(ZB):
            plane_rows(u_ref, tx, c, i, g_ref[c, i])

    def body(c, carry):
        forward(c)
        backward(c - 1)
        return carry

    forward(0)
    lax.fori_loop(1, channels, body, 0)
    backward(channels - 1)
    column_sums(u_ref, rt_ref, p_ref, channels)
    add_depth(p_ref, tz_ref, ph_ref, acc_ref, back_ref, factor)


def middle(spectra, field, plane, coefs, scale, shift, rt, bd, tx, txt, tz, ts, phase, factor):
    channels, planes, rows, grid_len = field.shape
    width = 2 * KZ * KXY
    volume = pl.BlockSpec((channels, ZB, rows, grid_len), lambda b: (0, b, 0, 0))
    return pl.pallas_call(
        functools.partial(middle_kernel, channels, factor),
        grid=(planes // ZB,),
        in_specs=[
            whole(spectra),
            volume,
            pl.BlockSpec((ZB, rows, grid_len), lambda b: (b, 0, 0)),
            scalars(),
            whole(scale),
            whole(shift),
            whole(rt),
            whole(bd),
            whole(tx),
            whole(txt),
            pl.BlockSpec((1,) + tz.shape[1:], lambda b: (b, 0, 0)),
            pl.BlockSpec((1,) + ts.shape[1:], lambda b: (b, 0, 0)),
            whole(phase),
        ],
        out_specs=[volume, volume, pl.BlockSpec((channels * KXY, width), lambda b: (0, 0))],
        out_shape=[jax.ShapeDtypeStruct(field.shape, BF16)] * 2
        + [jax.ShapeDtypeStruct((channels * KXY, width), BF16)],
        scratch_shapes=[
            pltpu.VMEM((channels * KXY, width), F32),
            pltpu.VMEM((channels * KXY, 2 * HALF), BF16),
            pltpu.VMEM((ZB, channels * 2 * KXY, grid_len), BF16),
            pltpu.VMEM((channels * KXY, 2 * HALF), BF16),
            pltpu.VMEM((channels * KXY, width), BF16),
            pltpu.VMEM((channels, rows, 2 * HALF), BF16),
        ],
        compiler_params=pltpu.CompilerParams(vmem_limit_bytes=VMEM),
        cost_estimate=pl.CostEstimate(
            flops=1024 * field.size, bytes_accessed=6 * field.size, transcendentals=field.size
        ),
        name="middle",
    )(spectra, field, plane, coefs, scale, shift, rt, bd, tx, txt, tz, ts, phase)


def finish_kernel(channels, q_ref, g_ref, gain_ref, bd_ref, txt_ref, ts_ref, ph_ref, o_ref, zz_ref, turned_ref, x_ref):
    turn_spectra(q_ref, ph_ref, turned_ref)
    zz_ref[...] = dot(turned_ref[...], ts_ref[0]).astype(BF16)
    txt = txt_ref[...]

    def columns(c, carry):
        x_ref[c] = column_fields(zz_ref, txt, c)
        return carry

    lax.fori_loop(0, channels, columns, 0, unroll=min(channels, 4))

    def body(c, carry):
        gain = gain_ref[c].astype(F32)
        for i in range(ZB):
            spatial = dot(x_ref[c], bd_ref[i])
            o_ref[c, i] = (spatial + gain * g_ref[c, i].astype(F32)).astype(BF16)
        return carry

    lax.fori_loop(0, channels, body, 0)


def finish(spectra, grads, gain, bd, txt, ts, phase):
    channels, planes, rows, grid_len = grads.shape
    width = 2 * KZ * KXY
    volume = pl.BlockSpec((channels, ZB, rows, grid_len), lambda b: (0, b, 0, 0))
    return pl.pallas_call(
        functools.partial(finish_kernel, channels),
        grid=(planes // ZB,),
        in_specs=[
            whole(spectra),
            volume,
            scalars(),
            whole(bd),
            whole(txt),
            pl.BlockSpec((1,) + ts.shape[1:], lambda b: (b, 0, 0)),
            whole(phase),
        ],
        out_specs=volume,
        out_shape=jax.ShapeDtypeStruct(grads.shape, BF16),
        scratch_shapes=[
            pltpu.VMEM((channels * KXY, 2 * HALF), BF16),
            pltpu.VMEM((channels * KXY, width), BF16),
            pltpu.VMEM((channels, rows, 2 * HALF), BF16),
        ],
        compiler_params=pltpu.CompilerParams(vmem_limit_bytes=VMEM),
        cost_estimate=pl.CostEstimate(
            flops=512 * grads.size, bytes_accessed=4 * grads.size, transcendentals=0
        ),
        name="finish",
    )(spectra, grads, gain, bd, txt, ts, phase)


def depth_mask(lanes):
    depth = lax.broadcasted_iota(jnp.int32, (KZ, 1, lanes), 0)
    lane = lax.broadcasted_iota(jnp.int32, (KZ, 1, lanes), 2)
    return (lane % KZ == depth).astype(F32)


def spread(sums, table, mask, channels):
    out = dot(sums, table)
    out = out.reshape(2, KZ, channels, out.shape[-1]) * mask[None]
    return jnp.sum(out, axis=1)


def gather_depth(values, table_t, mask):
    parts, channels, lanes = values.shape
    out = (values[:, None] * mask[None]).reshape(parts * KZ * channels, lanes)
    return dot(out.astype(BF16), table_t)


LANES = 512


def mix_kernel(groups, s_ref, w_ref, e_ref, o_ref):
    channels, outs, length = w_ref.shape[1:]
    own = outs // groups
    mask = depth_mask(LANES)
    per = SLOTS * KZ // LANES

    def body(k, carry):
        slot = pl.multiple_of(k // per * SLOTS, SLOTS)
        part = pl.multiple_of(k % per * LANES, LANES)
        lane = pl.multiple_of(k * LANES, LANES)
        u = spread(s_ref[:, pl.ds(slot, SLOTS)], e_ref[:, pl.ds(part, LANES)], mask, channels)
        real = jnp.zeros((outs, LANES), F32)
        imag = jnp.zeros((outs, LANES), F32)
        for c in range(channels):
            w0 = w_ref[0, c, :, pl.ds(lane, LANES)].astype(F32)
            w1 = w_ref[1, c, :, pl.ds(lane, LANES)].astype(F32)
            ur, ui = u[0, c : c + 1], u[1, c : c + 1]
            real += w0 * ur - w1 * ui
            imag += w1 * ur + w0 * ui
        for g in range(groups):
            o_ref[g, 0, :, pl.ds(lane, LANES)] = real[g * own : (g + 1) * own].astype(BF16)
            o_ref[g, 1, :, pl.ds(lane, LANES)] = imag[g * own : (g + 1) * own].astype(BF16)
        return carry

    lax.fori_loop(0, length // LANES, body, 0)


def mix(sums, weights, table, groups):
    _, channels, outs, length = weights.shape
    return pl.pallas_call(
        functools.partial(mix_kernel, groups),
        out_shape=jax.ShapeDtypeStruct((groups, 2, outs // groups, length), BF16),
        compiler_params=pltpu.CompilerParams(vmem_limit_bytes=VMEM),
        cost_estimate=pl.CostEstimate(
            flops=4 * weights.size, bytes_accessed=2 * weights.size, transcendentals=0
        ),
        name="mix",
    )(sums, weights, table)


def compress_kernel(p_ref, et_ref, o_ref):
    width = SLOTS * KZ
    mask = depth_mask(width)
    lane = lax.broadcasted_iota(jnp.int32, (1, 1, width), 2)
    twice = jnp.where(lane % KZ == 0, 1.0, 2.0).astype(F32)
    for k in range(p_ref.shape[-1] // width):
        part = p_ref[0, :, :, k * width : (k + 1) * width].astype(F32)
        for g in range(1, p_ref.shape[0]):
            part += p_ref[g, :, :, k * width : (k + 1) * width].astype(F32)
        out = gather_depth(part * twice, et_ref[...], mask)
        o_ref[:, k * SLOTS : (k + 1) * SLOTS] = out.astype(BF16)


def compress(parts, table_t):
    _, _, channels, length = parts.shape
    return pl.pallas_call(
        compress_kernel,
        out_shape=jax.ShapeDtypeStruct((2 * KZ * channels, length // KZ), BF16),
        compiler_params=pltpu.CompilerParams(vmem_limit_bytes=VMEM),
        name="compress",
    )(parts, table_t)


def unmix_kernel(s_ref, w_ref, e_ref, et_ref, o_ref, adj_ref):
    channels, outs, length = w_ref.shape[1:]
    groups = s_ref.shape[0]
    mask = depth_mask(LANES)
    per = SLOTS * KZ // LANES
    wide = depth_mask(SLOTS * KZ)

    def chunk(k, carry):
        def body(j, inner):
            slot = pl.multiple_of(k * SLOTS, SLOTS)
            part = pl.multiple_of(j * LANES, LANES)
            lane = pl.multiple_of(k * SLOTS * KZ + j * LANES, LANES)
            table = e_ref[:, pl.ds(part, LANES)]
            pieces = [spread(s_ref[g, :, pl.ds(slot, SLOTS)], table, mask, outs // groups) for g in range(groups)]
            gr = jnp.concatenate([piece[0] for piece in pieces], 0)
            gi = jnp.concatenate([piece[1] for piece in pieces], 0)
            for c in range(channels):
                w0 = w_ref[0, c, :, pl.ds(lane, LANES)].astype(F32)
                w1 = w_ref[1, c, :, pl.ds(lane, LANES)].astype(F32)
                adj_ref[0, c : c + 1, pl.ds(part, LANES)] = jnp.sum(w0 * gr + w1 * gi, axis=0, keepdims=True)
                adj_ref[1, c : c + 1, pl.ds(part, LANES)] = jnp.sum(w0 * gi - w1 * gr, axis=0, keepdims=True)
            return inner

        lax.fori_loop(0, per, body, 0)
        out = gather_depth(adj_ref[...], et_ref[...], wide)
        o_ref[:, pl.ds(pl.multiple_of(k * SLOTS, SLOTS), SLOTS)] = out.astype(BF16)
        return carry

    lax.fori_loop(0, length // (SLOTS * KZ), chunk, 0)


def unmix(sums, weights, table, table_t):
    _, channels, outs, length = weights.shape
    return pl.pallas_call(
        unmix_kernel,
        out_shape=jax.ShapeDtypeStruct((2 * KZ * channels, length // KZ), BF16),
        scratch_shapes=[pltpu.VMEM((2, channels, SLOTS * KZ), F32)],
        compiler_params=pltpu.CompilerParams(vmem_limit_bytes=VMEM),
        cost_estimate=pl.CostEstimate(
            flops=4 * weights.size, bytes_accessed=2 * weights.size, transcendentals=0
        ),
        name="unmix",
    )(sums, weights, table, table_t)


def per_device(field, forcing, slot_column, w_spec, skip_gain, bias):
    channels, planes, grid_len, _ = field.shape
    slabs, capacity = slot_column.shape
    groups = lax.axis_size("chan")
    own_rows = forcing.shape[1]
    factor = float(grid_len) ** -1.5
    columns = KXY * KXY

    row_np, col_np = plane_tables(grid_len)
    depth_np = depth_tables(planes, grid_len)
    rt = jnp.asarray(half_width(row_np))
    bd = jnp.asarray(half_width(np.swapaxes(row_np, 1, 2)) * ml_dtypes.bfloat16(factor))
    tx = jnp.asarray(half_width(col_np))
    txt = jnp.asarray(half_width(col_np.T))
    tz = jnp.asarray(half_width(depth_np))
    ts = jnp.asarray(half_width(np.swapaxes(depth_np, 1, 2)))
    table = jnp.asarray(half_width(spread_table()))
    table_t = jnp.asarray(half_width(spread_table().T))
    first = np.arange(slabs)[:, None] * planes * np.arange(KZ)[None, :] % grid_len
    first = np.repeat(first * (2.0 * math.pi / grid_len), KXY, axis=1)
    phases = jnp.asarray(np.stack([np.cos(first), np.sin(first)], 1).astype(np.float32))
    phase = lax.dynamic_index_in_dim(phases, lax.axis_index("slab"), 0, keepdims=False)

    numbers = jnp.arange(columns, dtype=jnp.int32)
    to_slots = (numbers[:, None] == slot_column.reshape(1, -1)).astype(BF16)
    to_columns = (slot_column.reshape(-1, 1) == numbers[None, :]).astype(BF16)

    plane = lax.all_gather(forcing, "chan", axis=1, tiled=True)

    def send_sums(coefs):
        by_slot = dot(
            coefs.reshape(channels, KXY, 2 * KZ, KXY).transpose(2, 0, 1, 3).reshape(-1, columns), to_slots
        ).astype(BF16)
        by_slot = by_slot.reshape(-1, slabs, capacity).transpose(1, 0, 2)
        parts = lax.all_to_all(by_slot, "slab", split_axis=0, concat_axis=0, tiled=True)
        return jnp.sum(parts.astype(F32), axis=0)

    def spread_spectra(own):
        everywhere = lax.all_gather(own, "slab", axis=0)
        by_column = jnp.einsum(
            "srk,skn->rn", everywhere, to_columns.reshape(slabs, capacity, columns), preferred_element_type=F32
        ).astype(BF16)
        by_column = by_column.reshape(2 * KZ, channels, KXY, KXY).transpose(1, 2, 0, 3)
        return by_column.reshape(channels * KXY, 2 * KZ * KXY)

    tx_own = lax.dynamic_slice_in_dim(tx, lax.axis_index("chan") * own_rows, own_rows, 1)
    forced = analyse(forcing[None], rt, tx_own, tz, phase, factor)
    forced = lax.psum(forced, "chan").astype(F32)
    coefs = analyse(field, rt, tx, tz, phase, factor).astype(F32)
    coefs = (coefs.reshape(channels, KXY, -1) + forced[None]).astype(BF16)
    sums = send_sums(coefs).astype(BF16)
    partial = mix(sums, w_spec, table, groups)
    parts = lax.all_to_all(partial, "chan", split_axis=0, concat_axis=0, tiled=True)
    spectra = spread_spectra(compress(parts, table_t))

    gain_rows = jnp.repeat(skip_gain, KXY)[:, None]
    centre = np.zeros((KXY, 2, ZB, KXY), np.float32)
    centre[KXY // 2, 0, :, KXY // 2] = 1.0 / factor
    centre = jnp.asarray(np.tile(centre.reshape(KXY, 2 * HALF), (channels, 1)))
    shift = centre * jnp.repeat(bias / skip_gain, KXY)[:, None]
    coefs_gelu = jnp.stack(
        [skip_gain**3 * (C1 * C2), skip_gain * C1, skip_gain * 0.5, skip_gain**2 * (6.0 * C1 * C2)], 1
    )
    output, grads, back = middle(
        spectra, field, plane, coefs_gelu, 1.0 / gain_rows, shift, rt, bd, tx, txt, tz, ts, phase, 0.5 * factor
    )
    doubling = jnp.where(jnp.arange(KZ) == 0, 1.0, 2.0).astype(F32)
    doubling = jnp.tile(jnp.repeat(doubling, channels), 2)[:, None]
    sums = (send_sums(back) * doubling).astype(BF16)
    everyone = lax.all_gather(sums, "chan", axis=0)
    adjoint = spread_spectra(unmix(everyone, w_spec, table, table_t))
    gradient = finish(adjoint, grads, skip_gain * 0.5, bd, txt, ts, phase)
    return output, gradient


def solution(mesh):
    placed = (
        P("chan", "slab", None, None),
        P("slab", "chan", None),
        P(),
        P(None, "chan", None, "slab"),
        P("chan"),
        P("chan"),
    )
    return jax.shard_map(
        per_device,
        mesh=mesh,
        in_specs=placed,
        out_specs=(P("chan", "slab", None, None), P("chan", "slab", None, None)),
        check_vma=False,
    )
```

```python
import functools
import math

import jax
import jax.numpy as jnp
import ml_dtypes
import numpy as np
from jax import lax
from jax.experimental import pallas as pl
from jax.experimental.pallas import tpu as pltpu
from jax.sharding import PartitionSpec as P

KXY = 32
KZ = 16
ZB = 4
HALF = ZB * KXY
C1 = math.sqrt(2.0 / math.pi)
C2 = 0.044715
F32 = jnp.float32
BF16 = jnp.bfloat16
SLOTS = 128
SMALL = 16 * 2**20
LARGE = 42 * 2**20


def dot(a, b):
    return jnp.dot(a, b, preferred_element_type=F32)


def angles(freqs, count, grid_len):
    turns = (freqs[:, None] * np.arange(count)[None, :]) % grid_len
    return turns * (2.0 * math.pi / grid_len)


def half_width(table):
    return table.astype(ml_dtypes.bfloat16)


def plane_tables(grid_len):
    angle = angles(np.arange(KXY) - KXY // 2, grid_len, grid_len)
    cosine, sine = np.cos(angle), np.sin(angle)
    rows = np.zeros((ZB, grid_len, 2, ZB, KXY))
    for i in range(ZB):
        rows[i, :, 0, i, :] = cosine.T
        rows[i, :, 1, i, :] = -sine.T
    rows = rows.reshape(ZB, grid_len, 2 * HALF)
    return rows, np.concatenate([cosine, sine], 0)


def depth_tables(planes, grid_len):
    angle = angles(np.arange(KZ), planes, grid_len)
    cosine, sine = np.cos(angle), np.sin(angle)
    table = np.zeros((planes // ZB, 2, ZB, KXY, 2, KZ, KXY))
    for b in range(planes // ZB):
        for i in range(ZB):
            for j in range(KXY):
                table[b, 0, i, j, 0, :, j] = cosine[:, b * ZB + i]
                table[b, 1, i, j, 0, :, j] = sine[:, b * ZB + i]
                table[b, 0, i, j, 1, :, j] = -sine[:, b * ZB + i]
                table[b, 1, i, j, 1, :, j] = cosine[:, b * ZB + i]
    return table.reshape(planes // ZB, 2 * HALF, 2 * KZ * KXY)


def spread_table():
    return np.repeat(np.eye(SLOTS), KZ, axis=1)


def whole(array):
    return pl.BlockSpec(array.shape, lambda *_: (0,) * len(array.shape))


def scalars():
    return pl.BlockSpec(memory_space=pltpu.SMEM)


def column_sums(u_ref, rt_ref, p_ref, first, last):
    rows = slice(first * 2 * KXY, last * 2 * KXY)
    total = dot(u_ref[0, rows], rt_ref[0])
    for i in range(1, ZB):
        total += dot(u_ref[i, rows], rt_ref[i])
    total = total.reshape(last - first, 2 * KXY, 2 * HALF)
    low, high = total[:, :KXY], total[:, KXY:]
    real = low[:, :, :HALF] + high[:, :, HALF:]
    imag = low[:, :, HALF:] - high[:, :, :HALF]
    rows = slice(first * KXY, last * KXY)
    p_ref[rows, :HALF] = real.reshape(-1, HALF).astype(BF16)
    p_ref[rows, HALF:] = imag.reshape(-1, HALF).astype(BF16)


def store_turned(total, ph_ref, out_ref, factor):
    half = KZ * KXY
    cosine, sine = ph_ref[0:1, :], ph_ref[1:2, :]
    real, imag = total[:, :half], total[:, half:]
    out_ref[:, :half] = ((real * cosine + imag * sine) * factor).astype(BF16)
    out_ref[:, half:] = ((imag * cosine - real * sine) * factor).astype(BF16)


def turn_spectra(q_ref, ph_ref, turned_ref):
    half = KZ * KXY
    cosine, sine = ph_ref[0:1, :], ph_ref[1:2, :]
    real, imag = q_ref[:, :half].astype(F32), q_ref[:, half:].astype(F32)
    turned_ref[:, :half] = (real * cosine - imag * sine).astype(BF16)
    turned_ref[:, half:] = (real * sine + imag * cosine).astype(BF16)


def resident():
    return pl.BlockSpec(memory_space=pltpu.VMEM)


def anywhere():
    return pl.BlockSpec(memory_space=pl.ANY)


def column_fields(zz_ref, txt, c):
    low = zz_ref[c * KXY : (c + 1) * KXY, :]
    high = jnp.concatenate([-low[:, HALF:], low[:, :HALF]], 1)
    return dot(txt, jnp.concatenate([low, high], 0)).astype(BF16)


def plane_rows(u_ref, tx, c, i, plane):
    u_ref[i, c * 2 * KXY : (c + 1) * 2 * KXY, :] = dot(tx, plane).astype(BF16)


def fetch_block(v_ref, kept_ref, sems, b):
    slot = lax.rem(b, kept_ref.shape[0])
    return pltpu.make_async_copy(v_ref.at[:, pl.ds(b * ZB, ZB)], kept_ref.at[slot], sems.at[slot])


def analyse_kernel(factor, v_ref, rt_ref, tx_ref, tz_ref, ph_ref, out_ref, acc_ref, p_ref, u_ref, kept_ref, sems):
    channels, planes = v_ref.shape[:2]
    blocks = planes // ZB
    half = channels // 2
    ahead = kept_ref.shape[0] - 1
    for b in range(ahead):
        fetch_block(v_ref, kept_ref, sems, b).start()
    tx = tx_ref[...]
    acc_ref[...] = jnp.zeros_like(acc_ref)

    def body(b, carry):
        @pl.when(b + ahead < blocks)
        def _():
            fetch_block(v_ref, kept_ref, sems, b + ahead).start()

        fetch_block(v_ref, kept_ref, sems, b).wait()
        slot = lax.rem(b, ahead + 1)
        for c in range(channels):
            for i in range(ZB):
                plane_rows(u_ref, tx, c, i, kept_ref[slot, c, i])
            if c == channels - 2:
                column_sums(u_ref, rt_ref, p_ref, 0, half)
        column_sums(u_ref, rt_ref, p_ref, half, channels)
        acc_ref[...] += dot(p_ref[...], tz_ref[b])
        return carry

    lax.fori_loop(0, blocks, body, 0)
    store_turned(acc_ref[...], ph_ref, out_ref, factor)


def analyse(volume, rt, tx, tz, phase, factor):
    channels, planes, rows, grid_len = volume.shape
    width = 2 * KZ * KXY
    return pl.pallas_call(
        functools.partial(analyse_kernel, factor),
        in_specs=[anywhere()] + [resident()] * 4,
        out_specs=resident(),
        out_shape=jax.ShapeDtypeStruct((channels * KXY, width), BF16),
        scratch_shapes=[
            pltpu.VMEM((channels * KXY, width), F32),
            pltpu.VMEM((channels * KXY, 2 * HALF), BF16),
            pltpu.VMEM((ZB, channels * 2 * KXY, grid_len), BF16),
            pltpu.VMEM((3, channels, ZB, rows, grid_len), BF16),
            pltpu.SemaphoreType.DMA((3,)),
        ],
        compiler_params=pltpu.CompilerParams(vmem_limit_bytes=LARGE),
        cost_estimate=pl.CostEstimate(
            flops=512 * volume.size, bytes_accessed=2 * volume.size, transcendentals=0
        ),
        name="analyse",
    )(volume, rt, tx, tz, phase)


def forced_kernel(factor, v_ref, rt_ref, tx_ref, tz_ref, ph_ref, out_ref, p_ref, u_ref):
    tx = tx_ref[...]
    blocks = v_ref.shape[0] // ZB
    for b in range(blocks):
        for i in range(ZB):
            plane_rows(u_ref, tx, b, i, v_ref[b * ZB + i])
    column_sums(u_ref, rt_ref, p_ref, 0, blocks)
    total = dot(p_ref[:KXY], tz_ref[0])
    for b in range(1, blocks):
        total += dot(p_ref[b * KXY : (b + 1) * KXY], tz_ref[b])
    store_turned(total, ph_ref, out_ref, factor)


def analyse_forced(forcing, rt, tx, tz, phase, factor):
    planes, _, grid_len = forcing.shape
    blocks = planes // ZB
    return pl.pallas_call(
        functools.partial(forced_kernel, factor),
        out_shape=jax.ShapeDtypeStruct((KXY, 2 * KZ * KXY), BF16),
        scratch_shapes=[
            pltpu.VMEM((blocks * KXY, 2 * HALF), BF16),
            pltpu.VMEM((ZB, blocks * 2 * KXY, grid_len), BF16),
        ],
        compiler_params=pltpu.CompilerParams(vmem_limit_bytes=SMALL),
        name="forced",
    )(forcing, rt, tx, tz, phase)


def gelu_planes(field, coefs_ref, c):
    cubic, linear, half, square = (coefs_ref[c, k].astype(BF16) for k in range(4))
    squared = field * field
    inner = field * (squared * cubic + linear)
    tangent = jnp.tanh(inner.astype(F32))
    upper = (1.0 + tangent).astype(BF16)
    lower = (1.0 - tangent).astype(BF16)
    value = field * (upper * half)
    slope = upper + value * lower * (squared * square + BF16(2.0 * C1))
    return value, value * slope


def send_half(buf_ref, o_ref, sems, b, h):
    half = buf_ref.shape[0] // 2
    part = pl.ds(h * half, half)
    return pltpu.make_async_copy(buf_ref.at[part], o_ref.at[part, pl.ds(b * ZB, ZB)], sems.at[h])


def fetch_forced(f_refs, raw_ref, sems, b, slot):
    return [
        pltpu.make_async_copy(ref.at[pl.ds(b * ZB, ZB)], raw_ref.at[slot, k], sems.at[slot, k])
        for k, ref in enumerate(f_refs)
    ]


def middle_kernel(factor, parts, *refs):
    q_ref, v_ref = refs[:2]
    f_refs = refs[2 : 2 + parts]
    (place_ref, coefs_ref, scale_ref, shift_ref, rt_ref, bd_ref, tx_ref, txt_ref, tz_ref, ts_ref, ph_ref) = refs[
        2 + parts : 13 + parts
    ]
    (o_ref, g_ref, back_ref, acc_ref, p_ref, u_ref, zz_ref, turned_ref, x_ref, f_ref, even_ref, odd_ref) = refs[
        13 + parts : 25 + parts
    ]
    kept_ref, buf_ref, grad_ref, raw_ref, out_sems, grad_sems, in_sems, v_sems = refs[25 + parts :]
    channels, planes = v_ref.shape[:2]
    blocks = planes // ZB
    half = channels // 2
    rows = raw_ref.shape[3]
    for copy in fetch_forced(f_refs, raw_ref, in_sems, 0, 0):
        copy.start()
    fetch_block(v_ref, kept_ref, v_sems, 0).start()
    turn_spectra(q_ref, ph_ref, turned_ref)
    acc_ref[...] = jnp.zeros_like(acc_ref)
    tx, txt = tx_ref[...], txt_ref[...]
    grads = (even_ref, odd_ref)

    def spatial(c, i):
        return dot(x_ref[c], bd_ref[i]).astype(BF16)

    def body(b, carry):
        slot = lax.rem(b, 2)

        @pl.when(b + 1 < blocks)
        def _():
            for copy in fetch_forced(f_refs, raw_ref, in_sems, b + 1, 1 - slot):
                copy.start()
            fetch_block(v_ref, kept_ref, v_sems, b + 1).start()

        for copy in fetch_forced(f_refs, raw_ref, in_sems, b, slot):
            copy.wait()
        for k in range(parts):
            f_ref[:, pl.ds(pl.multiple_of(place_ref[k] * rows, rows), rows), :] = raw_ref[slot, k]
        zz_ref[...] = (dot(turned_ref[...], ts_ref[b]) * scale_ref[...] + shift_ref[...]).astype(BF16)
        for c in range(channels):
            x_ref[c] = column_fields(zz_ref, txt, c)
        fetch_block(v_ref, kept_ref, v_sems, b).wait()
        for c in range(channels):
            if c % half == 0:

                @pl.when(b > 0)
                def _(c=c):
                    send_half(buf_ref, o_ref, out_sems, b - 1, c // half).wait()
                    send_half(grad_ref, g_ref, grad_sems, b - 1, c // half).wait()

            ahead = spatial(c, 0)
            for i in range(ZB):
                here = ahead
                if i < ZB - 1:
                    ahead = spatial(c, i + 1)
                if c > 0:
                    plane_rows(u_ref, tx, c - 1, i, grads[(c - 1) % 2][i])
                value, grad = gelu_planes(here + (kept_ref[slot, c, i] + f_ref[i]), coefs_ref, c)
                buf_ref[c, i] = value
                grad_ref[c, i] = grad
                grads[c % 2][i] = grad
            if c % half == half - 1:
                send_half(buf_ref, o_ref, out_sems, b, c // half).start()
                send_half(grad_ref, g_ref, grad_sems, b, c // half).start()
            if c == channels - 1:
                column_sums(u_ref, rt_ref, p_ref, 0, half)
        for i in range(ZB):
            plane_rows(u_ref, tx, channels - 1, i, grads[(channels - 1) % 2][i])
        column_sums(u_ref, rt_ref, p_ref, half, channels)
        acc_ref[...] += dot(p_ref[...], tz_ref[b])
        return carry

    lax.fori_loop(0, blocks, body, 0)
    store_turned(acc_ref[...], ph_ref, back_ref, factor)
    for h in range(2):
        send_half(buf_ref, o_ref, out_sems, blocks - 1, h).wait()
        send_half(grad_ref, g_ref, grad_sems, blocks - 1, h).wait()


def middle(spectra, kept, forced, place, coefs, scale, shift, rt, bd, tx, txt, tz, ts, phase, factor):
    channels, planes, rows, grid_len = kept.shape
    width = 2 * KZ * KXY
    parts = len(forced)
    return pl.pallas_call(
        functools.partial(middle_kernel, factor, parts),
        in_specs=[resident(), anywhere()] + [anywhere()] * parts + [scalars()] * 2 + [resident()] * 9,
        out_specs=[anywhere(), anywhere(), resident()],
        out_shape=[
            jax.ShapeDtypeStruct(kept.shape, BF16),
            jax.ShapeDtypeStruct(kept.shape, BF16),
            jax.ShapeDtypeStruct((channels * KXY, width), BF16),
        ],
        scratch_shapes=[
            pltpu.VMEM((channels * KXY, width), F32),
            pltpu.VMEM((channels * KXY, 2 * HALF), BF16),
            pltpu.VMEM((ZB, channels * 2 * KXY, grid_len), BF16),
            pltpu.VMEM((channels * KXY, 2 * HALF), BF16),
            pltpu.VMEM((channels * KXY, width), BF16),
            pltpu.VMEM((channels, rows, 2 * HALF), BF16),
            pltpu.VMEM((ZB, rows, grid_len), BF16),
            pltpu.VMEM((ZB, rows, grid_len), BF16),
            pltpu.VMEM((ZB, rows, grid_len), BF16),
            pltpu.VMEM((2, channels, ZB, rows, grid_len), BF16),
            pltpu.VMEM((channels, ZB, rows, grid_len), BF16),
            pltpu.VMEM((channels, ZB, rows, grid_len), BF16),
            pltpu.VMEM((2, parts, ZB) + forced[0].shape[1:], BF16),
            pltpu.SemaphoreType.DMA((2,)),
            pltpu.SemaphoreType.DMA((2,)),
            pltpu.SemaphoreType.DMA((2, parts)),
            pltpu.SemaphoreType.DMA((2,)),
        ],
        compiler_params=pltpu.CompilerParams(vmem_limit_bytes=LARGE),
        cost_estimate=pl.CostEstimate(
            flops=1024 * kept.size, bytes_accessed=2 * kept.size, transcendentals=kept.size
        ),
        name="middle",
    )(spectra, kept, *forced, place, coefs, scale, shift, rt, bd, tx, txt, tz, ts, phase)


def finish_kernel(q_ref, g_ref, gain_ref, bd_ref, txt_ref, ts_ref, ph_ref, o_ref, zz_ref, turned_ref, x_ref, kept_ref, buf_ref, sems, in_sems):
    channels, planes = g_ref.shape[:2]
    blocks = planes // ZB
    half = channels // 2
    ahead = kept_ref.shape[0] - 1
    for b in range(ahead):
        fetch_block(g_ref, kept_ref, in_sems, b).start()
    turn_spectra(q_ref, ph_ref, turned_ref)
    txt = txt_ref[...]

    def body(b, carry):
        @pl.when(b + ahead < blocks)
        def _():
            fetch_block(g_ref, kept_ref, in_sems, b + ahead).start()

        zz_ref[...] = dot(turned_ref[...], ts_ref[b]).astype(BF16)
        for c in range(channels):
            x_ref[c] = column_fields(zz_ref, txt, c)
        fetch_block(g_ref, kept_ref, in_sems, b).wait()
        slot = lax.rem(b, ahead + 1)
        for c in range(channels):
            if c % half == 0:

                @pl.when(b > 0)
                def _(c=c):
                    send_half(buf_ref, o_ref, sems, b - 1, c // half).wait()

            for i in range(ZB):
                plane = kept_ref[slot, c, i].astype(F32)
                buf_ref[c, i] = (dot(x_ref[c], bd_ref[i]) + gain_ref[c] * plane).astype(BF16)
            if c % half == half - 1:
                send_half(buf_ref, o_ref, sems, b, c // half).start()
        return carry

    lax.fori_loop(0, blocks, body, 0)
    for h in range(2):
        send_half(buf_ref, o_ref, sems, blocks - 1, h).wait()


def finish(spectra, grads, gain, bd, txt, ts, phase):
    channels, planes, rows, grid_len = grads.shape
    width = 2 * KZ * KXY
    return pl.pallas_call(
        finish_kernel,
        in_specs=[resident(), anywhere(), scalars()] + [resident()] * 4,
        out_specs=anywhere(),
        out_shape=jax.ShapeDtypeStruct(grads.shape, BF16),
        scratch_shapes=[
            pltpu.VMEM((channels * KXY, 2 * HALF), BF16),
            pltpu.VMEM((channels * KXY, width), BF16),
            pltpu.VMEM((channels, rows, 2 * HALF), BF16),
            pltpu.VMEM((3, channels, ZB, rows, grid_len), BF16),
            pltpu.VMEM((channels, ZB, rows, grid_len), BF16),
            pltpu.SemaphoreType.DMA((2,)),
            pltpu.SemaphoreType.DMA((3,)),
        ],
        compiler_params=pltpu.CompilerParams(vmem_limit_bytes=LARGE),
        cost_estimate=pl.CostEstimate(
            flops=512 * grads.size, bytes_accessed=2 * grads.size, transcendentals=0
        ),
        name="finish",
    )(spectra, grads, gain, bd, txt, ts, phase)


def depth_mask(lanes):
    depth = lax.broadcasted_iota(jnp.int32, (KZ, 1, lanes), 0)
    lane = lax.broadcasted_iota(jnp.int32, (KZ, 1, lanes), 2)
    return (lane % KZ == depth).astype(F32)


def spread(sums, table, mask, channels):
    out = dot(sums, table)
    out = out.reshape(2, KZ, channels, out.shape[-1]) * mask[None]
    return jnp.sum(out, axis=1)


def gather_depth(values, table_t, mask):
    parts, channels, lanes = values.shape
    out = (values[:, None] * mask[None]).reshape(parts * KZ * channels, lanes)
    return dot(out.astype(BF16), table_t)


LANES = 512


def mix_kernel(groups, s_ref, w_ref, e_ref, o_ref):
    channels, outs, length = w_ref.shape[1:]
    own = outs // groups
    mask = depth_mask(LANES)
    per = SLOTS * KZ // LANES

    def body(k, carry):
        slot = pl.multiple_of(k // per * SLOTS, SLOTS)
        part = pl.multiple_of(k % per * LANES, LANES)
        lane = pl.multiple_of(k * LANES, LANES)
        u = spread(s_ref[:, pl.ds(slot, SLOTS)], e_ref[:, pl.ds(part, LANES)], mask, channels)
        real = jnp.zeros((outs, LANES), F32)
        imag = jnp.zeros((outs, LANES), F32)
        for c in range(channels):
            w0 = w_ref[0, c, :, pl.ds(lane, LANES)].astype(F32)
            w1 = w_ref[1, c, :, pl.ds(lane, LANES)].astype(F32)
            ur, ui = u[0, c : c + 1], u[1, c : c + 1]
            real += w0 * ur - w1 * ui
            imag += w1 * ur + w0 * ui
        for g in range(groups):
            o_ref[g, 0, :, pl.ds(lane, LANES)] = real[g * own : (g + 1) * own].astype(BF16)
            o_ref[g, 1, :, pl.ds(lane, LANES)] = imag[g * own : (g + 1) * own].astype(BF16)
        return carry

    lax.fori_loop(0, length // LANES, body, 0)


def mix(sums, weights, table, groups):
    _, channels, outs, length = weights.shape
    return pl.pallas_call(
        functools.partial(mix_kernel, groups),
        out_shape=jax.ShapeDtypeStruct((groups, 2, outs // groups, length), BF16),
        compiler_params=pltpu.CompilerParams(vmem_limit_bytes=SMALL),
        cost_estimate=pl.CostEstimate(
            flops=4 * weights.size, bytes_accessed=2 * weights.size, transcendentals=0
        ),
        name="mix",
    )(sums, weights, table)


def compress_kernel(a_ref, b_ref, et_ref, o_ref):
    width = SLOTS * KZ
    mask = depth_mask(width)
    lane = lax.broadcasted_iota(jnp.int32, (1, 1, width), 2)
    twice = jnp.where(lane % KZ == 0, 1.0, 2.0).astype(F32)
    for k in range(a_ref.shape[-1] // width):
        lanes = slice(k * width, (k + 1) * width)
        total = a_ref[:, :, lanes].astype(F32) + b_ref[:, :, lanes].astype(F32)
        out = gather_depth(total * twice, et_ref[...], mask)
        o_ref[:, k * SLOTS : (k + 1) * SLOTS] = out.astype(BF16)


def compress(kept, got, table_t):
    _, channels, length = kept.shape
    return pl.pallas_call(
        compress_kernel,
        out_shape=jax.ShapeDtypeStruct((2 * KZ * channels, length // KZ), BF16),
        compiler_params=pltpu.CompilerParams(vmem_limit_bytes=SMALL),
        name="compress",
    )(kept, got, table_t)


def unmix_kernel(s_ref, w_ref, e_ref, et_ref, o_ref, adj_ref):
    channels, outs, length = w_ref.shape[1:]
    groups = s_ref.shape[0]
    mask = depth_mask(LANES)
    per = SLOTS * KZ // LANES
    wide = depth_mask(SLOTS * KZ)

    def chunk(k, carry):
        def body(j, inner):
            slot = pl.multiple_of(k * SLOTS, SLOTS)
            part = pl.multiple_of(j * LANES, LANES)
            lane = pl.multiple_of(k * SLOTS * KZ + j * LANES, LANES)
            table = e_ref[:, pl.ds(part, LANES)]
            pieces = [spread(s_ref[g, :, pl.ds(slot, SLOTS)], table, mask, outs // groups) for g in range(groups)]
            gr = jnp.concatenate([piece[0] for piece in pieces], 0)
            gi = jnp.concatenate([piece[1] for piece in pieces], 0)
            for c in range(channels):
                w0 = w_ref[0, c, :, pl.ds(lane, LANES)].astype(F32)
                w1 = w_ref[1, c, :, pl.ds(lane, LANES)].astype(F32)
                adj_ref[0, c : c + 1, pl.ds(part, LANES)] = jnp.sum(w0 * gr + w1 * gi, axis=0, keepdims=True)
                adj_ref[1, c : c + 1, pl.ds(part, LANES)] = jnp.sum(w0 * gi - w1 * gr, axis=0, keepdims=True)
            return inner

        lax.fori_loop(0, per, body, 0)
        out = gather_depth(adj_ref[...], et_ref[...], wide)
        o_ref[:, pl.ds(pl.multiple_of(k * SLOTS, SLOTS), SLOTS)] = out.astype(BF16)
        return carry

    lax.fori_loop(0, length // (SLOTS * KZ), chunk, 0)


def unmix(sums, weights, table, table_t):
    _, channels, outs, length = weights.shape
    return pl.pallas_call(
        unmix_kernel,
        out_shape=jax.ShapeDtypeStruct((2 * KZ * channels, length // KZ), BF16),
        scratch_shapes=[pltpu.VMEM((2, channels, SLOTS * KZ), F32)],
        compiler_params=pltpu.CompilerParams(vmem_limit_bytes=SMALL),
        cost_estimate=pl.CostEstimate(
            flops=4 * weights.size, bytes_accessed=2 * weights.size, transcendentals=0
        ),
        name="unmix",
    )(sums, weights, table, table_t)


def bits_of(count):
    return tuple(1 << k for k in reversed(range(count.bit_length() - 1)))


def offsets(route):
    found = [0]
    for bit in route:
        found = found + [k ^ bit for k in found]
    return found


def exchange(value, axis, offset):
    size = lax.axis_size(axis)
    return lax.ppermute(value, axis, [(k, k ^ offset) for k in range(size)])


def per_device(field, forcing, slot_column, w_spec, skip_gain, bias):
    channels, planes, grid_len, _ = field.shape
    slabs, capacity = slot_column.shape
    groups = lax.axis_size("chan")
    own_rows = forcing.shape[1]
    factor = float(grid_len) ** -1.5
    columns = KXY * KXY

    row_np, col_np = plane_tables(grid_len)
    depth_np = depth_tables(planes, grid_len)
    rt = jnp.asarray(half_width(row_np))
    bd = jnp.asarray(half_width(np.swapaxes(row_np, 1, 2)) * ml_dtypes.bfloat16(factor))
    tx = jnp.asarray(half_width(col_np))
    txt = jnp.asarray(half_width(col_np.T))
    tz = jnp.asarray(half_width(depth_np))
    ts = jnp.asarray(half_width(np.swapaxes(depth_np, 1, 2)))
    table = jnp.asarray(half_width(spread_table()))
    table_t = jnp.asarray(half_width(spread_table().T))
    first = np.arange(slabs)[:, None] * planes * np.arange(KZ)[None, :] % grid_len
    first = np.repeat(first * (2.0 * math.pi / grid_len), KXY, axis=1)
    phases = jnp.asarray(np.stack([np.cos(first), np.sin(first)], 1).astype(np.float32))
    phase = lax.dynamic_index_in_dim(phases, lax.axis_index("slab"), 0, keepdims=False)

    numbers = jnp.arange(columns, dtype=jnp.int32)
    to_slots = (numbers[:, None] == slot_column.reshape(1, -1)).astype(BF16)
    me_slab, me_chan = lax.axis_index("slab"), lax.axis_index("chan")
    slab_bits = bits_of(slabs)
    routes = (slab_bits, slab_bits[-1:] + slab_bits[:-1])
    from_slabs = [jnp.take(slot_column, me_slab ^ np.array(offsets(route)), axis=0) for route in routes]
    to_columns = [(table[:, :, None] == numbers).astype(BF16) for table in from_slabs]

    forced_parts = [forcing]
    for bit in bits_of(groups):
        forced_parts += [exchange(part, "chan", bit) for part in forced_parts]
    forced_places = (me_chan ^ np.array(offsets(bits_of(groups)))).astype(jnp.int32)

    def send_sums(coefs):
        by_slot = dot(
            coefs.reshape(channels, KXY, 2 * KZ, KXY).transpose(2, 0, 1, 3).reshape(-1, columns), to_slots
        ).astype(BF16)
        by_slot = by_slot.reshape(-1, slabs, capacity).transpose(1, 0, 2)
        parts = lax.all_to_all(by_slot, "slab", split_axis=0, concat_axis=0, tiled=True)
        return jnp.sum(parts.astype(F32), axis=0)

    def spread_spectra(own):
        pieces = [piece[None] for piece in jnp.split(own, 2, axis=0)]
        for step in range(len(slab_bits)):
            got = [exchange(piece, "slab", route[step]) for piece, route in zip(pieces, routes)]
            pieces = [jnp.concatenate(pair, 0) for pair in zip(pieces, got)]
        by_column = jnp.concatenate(
            [
                jnp.einsum("srk,skn->rn", piece, table, preferred_element_type=F32).astype(BF16)
                for piece, table in zip(pieces, to_columns)
            ],
            0,
        )
        by_column = by_column.reshape(2 * KZ, channels, KXY, KXY).transpose(1, 2, 0, 3)
        return by_column.reshape(channels * KXY, 2 * KZ * KXY)

    tx_own = lax.dynamic_slice_in_dim(tx, lax.axis_index("chan") * own_rows, own_rows, 1)
    forced = analyse_forced(forcing, rt, tx_own, tz, phase, factor)
    others = [exchange(forced, "chan", k) for k in range(1, groups)]
    coefs = analyse(field, rt, tx, tz, phase, factor)
    forced = sum(part.astype(F32) for part in [forced] + others)
    coefs = (coefs.astype(F32).reshape(channels, KXY, -1) + forced[None]).astype(BF16)
    sums = send_sums(coefs).astype(BF16)
    partial = mix(sums, w_spec, table, groups)
    for bit in reversed(bits_of(groups)):
        pairs = partial.reshape((partial.shape[0] // 2, 2) + partial.shape[1:])
        side = (me_chan // bit) % 2
        mine = lax.dynamic_index_in_dim(pairs, side, 1, keepdims=False)
        got = exchange(lax.dynamic_index_in_dim(pairs, 1 - side, 1, keepdims=False), "chan", bit)
        if mine.shape[0] > 1:
            partial = (mine.astype(F32) + got.astype(F32)).astype(BF16)
    spectra = spread_spectra(compress(mine[0], got[0], table_t))

    gain_rows = jnp.repeat(skip_gain, KXY)[:, None]
    centre = np.zeros((KXY, 2, ZB, KXY), np.float32)
    centre[KXY // 2, 0, :, KXY // 2] = 1.0 / factor
    centre = jnp.asarray(np.tile(centre.reshape(KXY, 2 * HALF), (channels, 1)))
    shift = centre * jnp.repeat(bias / skip_gain, KXY)[:, None]
    coefs_gelu = jnp.stack(
        [skip_gain**3 * (C1 * C2), skip_gain * C1, skip_gain * 0.5, skip_gain**2 * (6.0 * C1 * C2)], 1
    )
    output, grads, back = middle(
        spectra, field, forced_parts, forced_places, coefs_gelu, 1.0 / gain_rows, shift, rt, bd, tx, txt, tz, ts, phase, 0.5 * factor
    )
    doubling = jnp.where(jnp.arange(KZ) == 0, 1.0, 2.0).astype(F32)
    doubling = jnp.tile(jnp.repeat(doubling, channels), 2)[:, None]
    sums = (send_sums(back) * doubling).astype(BF16)
    everyone = lax.all_gather(sums, "chan", axis=0)
    adjoint = spread_spectra(unmix(everyone, w_spec, table, table_t))
    gradient = finish(adjoint, grads, skip_gain * 0.5, bd, txt, ts, phase)
    return output, gradient


def solution(mesh):
    placed = (
        P("chan", "slab", None, None),
        P("slab", "chan", None),
        P(),
        P(None, "chan", None, "slab"),
        P("chan"),
        P("chan"),
    )
    return jax.shard_map(
        per_device,
        mesh=mesh,
        in_specs=placed,
        out_specs=(P("chan", "slab", None, None), P("chan", "slab", None, None)),
        check_vma=False,
    )
```

```python
import functools
import math

import jax
import jax.numpy as jnp
import ml_dtypes
import numpy as np
from jax import lax
from jax.experimental import pallas as pl
from jax.experimental.pallas import tpu as pltpu
from jax.sharding import PartitionSpec as P

KXY = 32
KZ = 16
ZB = 4
HALF = ZB * KXY
C1 = math.sqrt(2.0 / math.pi)
C2 = 0.044715
F32 = jnp.float32
BF16 = jnp.bfloat16
SLOTS = 128
SMALL = 16 * 2**20
LARGE = 54 * 2**20


def dot(a, b):
    return jnp.dot(a, b, preferred_element_type=F32)


def angles(freqs, count, grid_len):
    turns = (freqs[:, None] * np.arange(count)[None, :]) % grid_len
    return turns * (2.0 * math.pi / grid_len)


def half_width(table):
    return table.astype(ml_dtypes.bfloat16)


def plane_tables(grid_len):
    angle = angles(np.arange(KXY) - KXY // 2, grid_len, grid_len)
    cosine, sine = np.cos(angle), np.sin(angle)
    rows = np.zeros((ZB, grid_len, 2, ZB, KXY))
    for i in range(ZB):
        rows[i, :, 0, i, :] = cosine.T
        rows[i, :, 1, i, :] = -sine.T
    rows = rows.reshape(ZB, grid_len, 2 * HALF)
    return rows, np.concatenate([cosine, sine], 0)


def depth_tables(planes, grid_len):
    angle = angles(np.arange(KZ), planes, grid_len)
    cosine, sine = np.cos(angle), np.sin(angle)
    table = np.zeros((planes // ZB, 2, ZB, KXY, 2, KZ, KXY))
    for b in range(planes // ZB):
        for i in range(ZB):
            for j in range(KXY):
                table[b, 0, i, j, 0, :, j] = cosine[:, b * ZB + i]
                table[b, 1, i, j, 0, :, j] = sine[:, b * ZB + i]
                table[b, 0, i, j, 1, :, j] = -sine[:, b * ZB + i]
                table[b, 1, i, j, 1, :, j] = cosine[:, b * ZB + i]
    return table.reshape(planes // ZB, 2 * HALF, 2 * KZ * KXY)


def spread_table():
    return np.repeat(np.eye(SLOTS), KZ, axis=1)


def whole(array):
    return pl.BlockSpec(array.shape, lambda *_: (0,) * len(array.shape))


def scalars():
    return pl.BlockSpec(memory_space=pltpu.SMEM)


def column_sums(u_ref, rt_ref, p_ref, first, last):
    rows = slice(first * 2 * KXY, last * 2 * KXY)
    total = dot(u_ref[0, rows], rt_ref[0])
    for i in range(1, ZB):
        total += dot(u_ref[i, rows], rt_ref[i])
    total = total.reshape(last - first, 2 * KXY, 2 * HALF)
    low, high = total[:, :KXY], total[:, KXY:]
    real = low[:, :, :HALF] + high[:, :, HALF:]
    imag = low[:, :, HALF:] - high[:, :, :HALF]
    rows = slice(first * KXY, last * KXY)
    p_ref[rows, :HALF] = real.reshape(-1, HALF).astype(BF16)
    p_ref[rows, HALF:] = imag.reshape(-1, HALF).astype(BF16)


def store_turned(total, ph_ref, out_ref, factor):
    half = KZ * KXY
    cosine, sine = ph_ref[0:1, :], ph_ref[1:2, :]
    real, imag = total[:, :half], total[:, half:]
    out_ref[:, :half] = ((real * cosine + imag * sine) * factor).astype(BF16)
    out_ref[:, half:] = ((imag * cosine - real * sine) * factor).astype(BF16)


def turn_spectra(q_ref, ph_ref, turned_ref):
    half = KZ * KXY
    cosine, sine = ph_ref[0:1, :], ph_ref[1:2, :]
    real, imag = q_ref[:, :half].astype(F32), q_ref[:, half:].astype(F32)
    turned_ref[:, :half] = (real * cosine - imag * sine).astype(BF16)
    turned_ref[:, half:] = (real * sine + imag * cosine).astype(BF16)


def resident():
    return pl.BlockSpec(memory_space=pltpu.VMEM)


def anywhere():
    return pl.BlockSpec(memory_space=pltpu.HBM)


def column_fields(zz_ref, txt, c):
    low = zz_ref[c * KXY : (c + 1) * KXY, :]
    high = jnp.concatenate([-low[:, HALF:], low[:, :HALF]], 1)
    return dot(txt, jnp.concatenate([low, high], 0)).astype(BF16)


def plane_rows(u_ref, tx, c, i, plane):
    u_ref[i, c * 2 * KXY : (c + 1) * 2 * KXY, :] = dot(tx, plane).astype(BF16)


def fetch_block(v_ref, kept_ref, sems, b):
    slot = lax.rem(b, kept_ref.shape[0])
    return pltpu.make_async_copy(v_ref.at[:, pl.ds(b * ZB, ZB)], kept_ref.at[slot], sems.at[slot])


def fetch_table(hbm_ref, table_ref, sems, b):
    slot = lax.rem(b, table_ref.shape[0])
    return pltpu.make_async_copy(hbm_ref.at[b], table_ref.at[slot], sems.at[slot])


def analyse_kernel(
    factor, v_ref, rt_ref, tx_ref, tz_hbm, ph_ref, out_ref, acc_ref, p_ref, u_ref, kept_ref, tz_ref, sems, tz_sems
):
    channels, planes = v_ref.shape[:2]
    blocks = planes // ZB
    half = channels // 2
    ahead = kept_ref.shape[0] - 1
    for b in range(ahead):
        fetch_block(v_ref, kept_ref, sems, b).start()
        fetch_table(tz_hbm, tz_ref, tz_sems, b).start()
    tx = tx_ref[...]
    acc_ref[...] = jnp.zeros_like(acc_ref)

    def body(b, carry):
        @pl.when(b + ahead < blocks)
        def _():
            fetch_block(v_ref, kept_ref, sems, b + ahead).start()
            fetch_table(tz_hbm, tz_ref, tz_sems, b + ahead).start()

        fetch_block(v_ref, kept_ref, sems, b).wait()
        slot = lax.rem(b, ahead + 1)
        for c in range(channels):
            for i in range(ZB):
                plane_rows(u_ref, tx, c, i, kept_ref[slot, c, i])
            if c == channels - 2:
                column_sums(u_ref, rt_ref, p_ref, 0, half)
        column_sums(u_ref, rt_ref, p_ref, half, channels)
        fetch_table(tz_hbm, tz_ref, tz_sems, b).wait()
        acc_ref[...] += dot(p_ref[...], tz_ref[slot])
        return carry

    lax.fori_loop(0, blocks, body, 0)
    store_turned(acc_ref[...], ph_ref, out_ref, factor)


def analyse(volume, rt, tx, tz, phase, factor):
    channels, planes, rows, grid_len = volume.shape
    width = 2 * KZ * KXY
    return pl.pallas_call(
        functools.partial(analyse_kernel, factor),
        in_specs=[anywhere(), resident(), resident(), anywhere(), resident()],
        out_specs=resident(),
        out_shape=jax.ShapeDtypeStruct((channels * KXY, width), BF16),
        scratch_shapes=[
            pltpu.VMEM((channels * KXY, width), F32),
            pltpu.VMEM((channels * KXY, 2 * HALF), BF16),
            pltpu.VMEM((ZB, channels * 2 * KXY, grid_len), BF16),
            pltpu.VMEM((3, channels, ZB, rows, grid_len), BF16),
            pltpu.VMEM((3,) + tz.shape[1:], BF16),
            pltpu.SemaphoreType.DMA((3,)),
            pltpu.SemaphoreType.DMA((3,)),
        ],
        compiler_params=pltpu.CompilerParams(vmem_limit_bytes=LARGE),
        cost_estimate=pl.CostEstimate(
            flops=512 * volume.size, bytes_accessed=2 * volume.size, transcendentals=0
        ),
        name="analyse",
    )(volume, rt, tx, tz, phase)


def forced_kernel(factor, v_ref, rt_ref, tx_ref, tz_hbm, ph_ref, out_ref, p_ref, u_ref, tz_ref, sem):
    tx = tx_ref[...]
    copy = pltpu.make_async_copy(tz_hbm, tz_ref, sem)
    copy.start()
    blocks = v_ref.shape[0] // ZB
    for b in range(blocks):
        for i in range(ZB):
            plane_rows(u_ref, tx, b, i, v_ref[b * ZB + i])
    column_sums(u_ref, rt_ref, p_ref, 0, blocks)
    copy.wait()
    total = dot(p_ref[:KXY], tz_ref[0])
    for b in range(1, blocks):
        total += dot(p_ref[b * KXY : (b + 1) * KXY], tz_ref[b])
    store_turned(total, ph_ref, out_ref, factor)


def analyse_forced(forcing, rt, tx, tz, phase, factor):
    planes, _, grid_len = forcing.shape
    blocks = planes // ZB
    return pl.pallas_call(
        functools.partial(forced_kernel, factor),
        in_specs=[resident(), resident(), resident(), anywhere(), resident()],
        out_shape=jax.ShapeDtypeStruct((KXY, 2 * KZ * KXY), BF16),
        scratch_shapes=[
            pltpu.VMEM((blocks * KXY, 2 * HALF), BF16),
            pltpu.VMEM((ZB, blocks * 2 * KXY, grid_len), BF16),
            pltpu.VMEM(tz.shape, BF16),
            pltpu.SemaphoreType.DMA,
        ],
        compiler_params=pltpu.CompilerParams(vmem_limit_bytes=SMALL),
        name="forced",
    )(forcing, rt, tx, tz, phase)


def gelu_planes(field, coefs_ref, c):
    cubic, linear, half, square = (coefs_ref[c, k].astype(BF16) for k in range(4))
    squared = field * field
    inner = field * (squared * cubic + linear)
    tangent = jnp.tanh(inner.astype(F32))
    upper = (1.0 + tangent).astype(BF16)
    lower = (1.0 - tangent).astype(BF16)
    value = field * (upper * half)
    slope = upper + value * lower * (squared * square + BF16(2.0 * C1))
    return value, value * slope


def send_block(buf_ref, o_ref, sems, b):
    slot = lax.rem(b, 2)
    return pltpu.make_async_copy(buf_ref.at[slot], o_ref.at[:, pl.ds(b * ZB, ZB)], sems.at[slot])


def fetch_forced(f_refs, raw_ref, sems, b, slot):
    return [
        pltpu.make_async_copy(ref.at[pl.ds(b * ZB, ZB)], raw_ref.at[slot, k], sems.at[slot, k])
        for k, ref in enumerate(f_refs)
    ]


def middle_kernel(factor, parts, *refs):
    q_ref, v_ref = refs[:2]
    f_refs = refs[2 : 2 + parts]
    (place_ref, coefs_ref, scale_ref, shift_ref, rt_ref, bd_ref, tx_ref, txt_ref, tz_hbm, ts_hbm, ph_ref) = refs[
        2 + parts : 13 + parts
    ]
    (o_ref, g_ref, back_ref, acc_ref, p_ref, u_ref, zz_ref, turned_ref, x_ref, f_ref, even_ref, odd_ref) = refs[
        13 + parts : 25 + parts
    ]
    kept_ref, buf_ref, grad_ref, raw_ref, tz_ref, ts_ref = refs[25 + parts : 31 + parts]
    out_sems, grad_sems, in_sems, v_sems, tz_sems, ts_sems = refs[31 + parts :]
    channels, planes = v_ref.shape[:2]
    blocks = planes // ZB
    half = channels // 2
    rows = raw_ref.shape[3]
    for copy in fetch_forced(f_refs, raw_ref, in_sems, 0, 0):
        copy.start()
    fetch_table(ts_hbm, ts_ref, ts_sems, 0).start()
    fetch_block(v_ref, kept_ref, v_sems, 0).start()
    fetch_table(tz_hbm, tz_ref, tz_sems, 0).start()
    turn_spectra(q_ref, ph_ref, turned_ref)
    acc_ref[...] = jnp.zeros_like(acc_ref)
    tx, txt = tx_ref[...], txt_ref[...]
    grads = (even_ref, odd_ref)

    def spatial(c, i):
        return dot(x_ref[c], bd_ref[i]).astype(BF16)

    def body(b, carry):
        slot = lax.rem(b, 2)

        @pl.when(b + 1 < blocks)
        def _():
            for copy in fetch_forced(f_refs, raw_ref, in_sems, b + 1, 1 - slot):
                copy.start()
            fetch_table(ts_hbm, ts_ref, ts_sems, b + 1).start()
            fetch_block(v_ref, kept_ref, v_sems, b + 1).start()
            fetch_table(tz_hbm, tz_ref, tz_sems, b + 1).start()

        for copy in fetch_forced(f_refs, raw_ref, in_sems, b, slot):
            copy.wait()
        fetch_table(ts_hbm, ts_ref, ts_sems, b).wait()
        fetch_block(v_ref, kept_ref, v_sems, b).wait()
        fetch_table(tz_hbm, tz_ref, tz_sems, b).wait()

        @pl.when(b > 1)
        def _():
            send_block(buf_ref, o_ref, out_sems, b - 2).wait()
            send_block(grad_ref, g_ref, grad_sems, b - 2).wait()

        for k in range(parts):
            f_ref[:, pl.ds(pl.multiple_of(place_ref[k] * rows, rows), rows), :] = raw_ref[slot, k]
        zz_ref[...] = (dot(turned_ref[...], ts_ref[slot]) * scale_ref[...] + shift_ref[...]).astype(BF16)
        for c in range(channels):
            x_ref[c] = column_fields(zz_ref, txt, c)
        for c in range(channels):
            ahead = spatial(c, 0)
            for i in range(ZB):
                here = ahead
                if i < ZB - 1:
                    ahead = spatial(c, i + 1)
                if c > 0:
                    plane_rows(u_ref, tx, c - 1, i, grads[(c - 1) % 2][i])
                value, grad = gelu_planes(here + (kept_ref[slot, c, i] + f_ref[i]), coefs_ref, c)
                buf_ref[slot, c, i] = value
                grad_ref[slot, c, i] = grad
                grads[c % 2][i] = grad
            if c == channels - 1:
                column_sums(u_ref, rt_ref, p_ref, 0, half)
        for i in range(ZB):
            plane_rows(u_ref, tx, channels - 1, i, grads[(channels - 1) % 2][i])
        column_sums(u_ref, rt_ref, p_ref, half, channels)
        acc_ref[...] += dot(p_ref[...], tz_ref[slot])
        send_block(buf_ref, o_ref, out_sems, b).start()
        send_block(grad_ref, g_ref, grad_sems, b).start()
        return carry

    lax.fori_loop(0, blocks, body, 0)
    store_turned(acc_ref[...], ph_ref, back_ref, factor)
    for b in (blocks - 2, blocks - 1):
        send_block(buf_ref, o_ref, out_sems, b).wait()
        send_block(grad_ref, g_ref, grad_sems, b).wait()


def middle(spectra, kept, forced, place, coefs, scale, shift, rt, bd, tx, txt, tz, ts, phase, factor):
    channels, planes, rows, grid_len = kept.shape
    width = 2 * KZ * KXY
    parts = len(forced)
    return pl.pallas_call(
        functools.partial(middle_kernel, factor, parts),
        in_specs=[resident(), anywhere()] + [anywhere()] * parts + [scalars()] * 2 + [resident()] * 6 + [anywhere()] * 2 + [resident()],
        out_specs=[anywhere(), anywhere(), resident()],
        out_shape=[
            jax.ShapeDtypeStruct(kept.shape, BF16),
            jax.ShapeDtypeStruct(kept.shape, BF16),
            jax.ShapeDtypeStruct((channels * KXY, width), BF16),
        ],
        scratch_shapes=[
            pltpu.VMEM((channels * KXY, width), F32),
            pltpu.VMEM((channels * KXY, 2 * HALF), BF16),
            pltpu.VMEM((ZB, channels * 2 * KXY, grid_len), BF16),
            pltpu.VMEM((channels * KXY, 2 * HALF), BF16),
            pltpu.VMEM((channels * KXY, width), BF16),
            pltpu.VMEM((channels, rows, 2 * HALF), BF16),
            pltpu.VMEM((ZB, rows, grid_len), BF16),
            pltpu.VMEM((ZB, rows, grid_len), BF16),
            pltpu.VMEM((ZB, rows, grid_len), BF16),
            pltpu.VMEM((2, channels, ZB, rows, grid_len), BF16),
            pltpu.VMEM((2, channels, ZB, rows, grid_len), BF16),
            pltpu.VMEM((2, channels, ZB, rows, grid_len), BF16),
            pltpu.VMEM((2, parts, ZB) + forced[0].shape[1:], BF16),
            pltpu.VMEM((2,) + tz.shape[1:], BF16),
            pltpu.VMEM((2,) + ts.shape[1:], BF16),
            pltpu.SemaphoreType.DMA((2,)),
            pltpu.SemaphoreType.DMA((2,)),
            pltpu.SemaphoreType.DMA((2, parts)),
            pltpu.SemaphoreType.DMA((2,)),
            pltpu.SemaphoreType.DMA((2,)),
            pltpu.SemaphoreType.DMA((2,)),
        ],
        compiler_params=pltpu.CompilerParams(vmem_limit_bytes=LARGE),
        cost_estimate=pl.CostEstimate(
            flops=1024 * kept.size, bytes_accessed=2 * kept.size, transcendentals=kept.size
        ),
        name="middle",
    )(spectra, kept, *forced, place, coefs, scale, shift, rt, bd, tx, txt, tz, ts, phase)


def finish_kernel(
    q_ref, g_ref, gain_ref, bd_ref, txt_ref, ts_hbm, ph_ref, o_ref, zz_ref, turned_ref, x_ref, kept_ref, buf_ref, ts_ref,
    sems, in_sems, ts_sems,
):
    channels, planes = g_ref.shape[:2]
    blocks = planes // ZB
    ahead = kept_ref.shape[0] - 1
    for b in range(ahead):
        fetch_table(ts_hbm, ts_ref, ts_sems, b).start()
        fetch_block(g_ref, kept_ref, in_sems, b).start()
    turn_spectra(q_ref, ph_ref, turned_ref)
    txt = txt_ref[...]

    def body(b, carry):
        @pl.when(b + ahead < blocks)
        def _():
            fetch_table(ts_hbm, ts_ref, ts_sems, b + ahead).start()
            fetch_block(g_ref, kept_ref, in_sems, b + ahead).start()

        slot = lax.rem(b, ahead + 1)
        fetch_table(ts_hbm, ts_ref, ts_sems, b).wait()
        fetch_block(g_ref, kept_ref, in_sems, b).wait()

        @pl.when(b > 1)
        def _():
            send_block(buf_ref, o_ref, sems, b - 2).wait()

        zz_ref[...] = dot(turned_ref[...], ts_ref[slot]).astype(BF16)
        for c in range(channels):
            x_ref[c] = column_fields(zz_ref, txt, c)
        for c in range(channels):
            for i in range(ZB):
                plane = kept_ref[slot, c, i].astype(F32)
                buf_ref[lax.rem(b, 2), c, i] = (dot(x_ref[c], bd_ref[i]) + gain_ref[c] * plane).astype(BF16)
        send_block(buf_ref, o_ref, sems, b).start()
        return carry

    lax.fori_loop(0, blocks, body, 0)
    for b in (blocks - 2, blocks - 1):
        send_block(buf_ref, o_ref, sems, b).wait()


def finish(spectra, grads, gain, bd, txt, ts, phase):
    channels, planes, rows, grid_len = grads.shape
    width = 2 * KZ * KXY
    return pl.pallas_call(
        finish_kernel,
        in_specs=[resident(), anywhere(), scalars(), resident(), resident(), anywhere(), resident()],
        out_specs=anywhere(),
        out_shape=jax.ShapeDtypeStruct(grads.shape, BF16),
        scratch_shapes=[
            pltpu.VMEM((channels * KXY, 2 * HALF), BF16),
            pltpu.VMEM((channels * KXY, width), BF16),
            pltpu.VMEM((channels, rows, 2 * HALF), BF16),
            pltpu.VMEM((3, channels, ZB, rows, grid_len), BF16),
            pltpu.VMEM((2, channels, ZB, rows, grid_len), BF16),
            pltpu.VMEM((3,) + ts.shape[1:], BF16),
            pltpu.SemaphoreType.DMA((2,)),
            pltpu.SemaphoreType.DMA((3,)),
            pltpu.SemaphoreType.DMA((3,)),
        ],
        compiler_params=pltpu.CompilerParams(vmem_limit_bytes=LARGE),
        cost_estimate=pl.CostEstimate(
            flops=512 * grads.size, bytes_accessed=2 * grads.size, transcendentals=0
        ),
        name="finish",
    )(spectra, grads, gain, bd, txt, ts, phase)


def depth_mask(lanes):
    depth = lax.broadcasted_iota(jnp.int32, (KZ, 1, lanes), 0)
    lane = lax.broadcasted_iota(jnp.int32, (KZ, 1, lanes), 2)
    return (lane % KZ == depth).astype(F32)


def spread(sums, table, mask, channels):
    out = dot(sums, table)
    out = out.reshape(2, KZ, channels, out.shape[-1]) * mask[None]
    return jnp.sum(out, axis=1)


def gather_depth(values, table_t, mask):
    parts, channels, lanes = values.shape
    out = (values[:, None] * mask[None]).reshape(parts * KZ * channels, lanes)
    return dot(out.astype(BF16), table_t)


LANES = 512
GROUP = 8
WIDE = GROUP * KXY


def iota(shape, axis):
    return lax.broadcasted_iota(jnp.int32, shape, axis)


def one_hot(hit):
    return jnp.where(hit, 1.0, 0.0).astype(BF16)


def row_order(channels):
    shape = (WIDE, channels * KXY)
    row, lane = iota(shape, 0), iota(shape, 1)
    return one_hot((row // GROUP == lane % KXY) & (row % GROUP == lane // KXY))


def row_order_back(channels):
    shape = (channels * KXY, WIDE)
    row, lane = iota(shape, 0), iota(shape, 1)
    return one_hot((lane // GROUP == row % KXY) & (lane % GROUP == row // KXY))


def chosen(slots_ref, k, columns):
    capacity = slots_ref.shape[-1]
    return one_hot(iota((columns, capacity), 0) == slots_ref[k])


def own_lanes():
    shape = (GROUP, 1, WIDE)
    return (iota(shape, 0) == iota(shape, 2) // KXY).astype(F32)


def to_slots_kernel(slots_ref, d_ref, *refs):
    others, (o_ref, t_ref) = refs[:-2], refs[-2:]
    channels = d_ref.shape[0] // KXY
    data = d_ref[...]
    if others:
        extra = others[0][...].astype(F32)
        for other in others[1:]:
            extra += other[...].astype(F32)
        data = data.astype(F32).reshape(channels, KXY, -1) + extra[None]
        data = data.reshape(channels * KXY, -1).astype(BF16)
    data = dot(row_order(channels), data).astype(BF16)
    row, lane = iota((WIDE, WIDE), 0), iota((WIDE, WIDE), 1)
    same = row % KXY == lane % KXY
    mask = own_lanes()
    groups = KXY // GROUP
    for m in range(GROUP):
        pick = one_hot(same & (row // KXY == m))
        for k in range(2 * KZ // GROUP):
            out = dot(data[:, k * WIDE : (k + 1) * WIDE], pick)
            out = jnp.sum(out.reshape(groups, GROUP, GROUP, WIDE) * mask[None], axis=1)
            first = (k * GROUP + m) * GROUP
            for g in range(groups):
                t_ref[first : first + GROUP, g * WIDE : (g + 1) * WIDE] = out[g]
    table = t_ref[...].astype(BF16)
    if channels < GROUP:
        shape = (2 * KZ * channels, WIDE)
        row, lane = iota(shape, 0), iota(shape, 1)
        keep = (row // channels == lane // GROUP) & (row % channels == lane % GROUP)
        table = dot(one_hot(keep), table).astype(BF16)
    for k in range(slots_ref.shape[0]):
        o_ref[k] = dot(table, chosen(slots_ref, k, KXY * KXY)).astype(BF16)


def to_slots(slots, coefs, others):
    slabs, _, capacity = slots.shape
    return pl.pallas_call(
        to_slots_kernel,
        out_shape=jax.ShapeDtypeStruct((slabs, coefs.shape[0], capacity), BF16),
        scratch_shapes=[pltpu.VMEM((WIDE, KXY * KXY), F32)],
        compiler_params=pltpu.CompilerParams(vmem_limit_bytes=SMALL),
        name="to_slots",
    )(slots, coefs, *others)


def to_columns_kernel(places, slots_ref, *refs):
    (a_refs, b_refs), (o_ref, t_ref) = (refs[:2], refs[2:4]), refs[4:]
    channels = o_ref.shape[0] // KXY
    columns = KXY * KXY
    half = slots_ref.shape[0] // 2

    def piece(pair, k):
        return pair[k // half][k % half]

    total = None
    for k, place in enumerate(places):
        both = jnp.concatenate([piece(a_refs, k), piece(b_refs, place)], 0)
        part = lax.dot_general(
            both, chosen(slots_ref, k, columns), (((1,), (1,)), ((), ())), preferred_element_type=F32
        )
        total = part if total is None else total + part
    if channels < GROUP:
        shape = (WIDE, 2 * KZ * channels)
        row, lane = iota(shape, 0), iota(shape, 1)
        keep = (lane // channels == row // GROUP) & (lane % channels == row % GROUP)
        total = dot(one_hot(keep), total.astype(BF16))
    t_ref[...] = total
    row, lane = iota((WIDE, WIDE), 0), iota((WIDE, WIDE), 1)
    same = row % KXY == lane % KXY
    mask = own_lanes()
    groups = KXY // GROUP
    back = row_order_back(channels)
    picks = [one_hot(same & (lane // KXY == m)) for m in range(GROUP)]
    for k in range(2 * KZ // GROUP):
        found = None
        for m in range(GROUP):
            first = (k * GROUP + m) * GROUP
            rows = t_ref[first : first + GROUP, :]
            parts = [(rows[None, :, g * WIDE : (g + 1) * WIDE] * mask).reshape(WIDE // groups, WIDE) for g in range(groups)]
            part = dot(jnp.concatenate(parts, 0).astype(BF16), picks[m])
            found = part if found is None else found + part
        o_ref[:, k * WIDE : (k + 1) * WIDE] = dot(back, found.astype(BF16)).astype(BF16)


def to_columns(slots, pieces, places, channels):
    return pl.pallas_call(
        functools.partial(to_columns_kernel, places),
        out_shape=jax.ShapeDtypeStruct((channels * KXY, 2 * KZ * KXY), BF16),
        scratch_shapes=[pltpu.VMEM((WIDE, KXY * KXY), F32)],
        compiler_params=pltpu.CompilerParams(vmem_limit_bytes=SMALL),
        name="to_columns",
    )(slots, *pieces)


def fetch_lanes(hbm_ref, w_ref, sems, k):
    lanes = pl.ds(k * LANES, LANES)
    return pltpu.make_async_copy(hbm_ref.at[:, :, :, lanes], w_ref.at[:, :, :, lanes], sems.at[k])


def mix_kernel(groups, p_ref, w_hbm, e_ref, o_ref, s_ref, w_ref, sems):
    channels, outs, length = w_ref.shape[1:]
    for k in range(length // LANES):
        fetch_lanes(w_hbm, w_ref, sems, k).start()
    own = outs // groups
    mask = depth_mask(LANES)
    per = SLOTS * KZ // LANES
    total = p_ref[0].astype(F32)
    for k in range(1, p_ref.shape[0]):
        total += p_ref[k].astype(F32)
    s_ref[...] = total.astype(BF16)

    def body(k, carry):
        slot = pl.multiple_of(k // per * SLOTS, SLOTS)
        part = pl.multiple_of(k % per * LANES, LANES)
        lane = pl.multiple_of(k * LANES, LANES)
        fetch_lanes(w_hbm, w_ref, sems, k).wait()
        u = spread(s_ref[:, pl.ds(slot, SLOTS)], e_ref[:, pl.ds(part, LANES)], mask, channels)
        real = jnp.zeros((outs, LANES), F32)
        imag = jnp.zeros((outs, LANES), F32)
        for c in range(channels):
            w0 = w_ref[0, c, :, pl.ds(lane, LANES)].astype(F32)
            w1 = w_ref[1, c, :, pl.ds(lane, LANES)].astype(F32)
            ur, ui = u[0, c : c + 1], u[1, c : c + 1]
            real += w0 * ur - w1 * ui
            imag += w1 * ur + w0 * ui
        for g in range(groups):
            o_ref[g, 0, :, pl.ds(lane, LANES)] = real[g * own : (g + 1) * own].astype(BF16)
            o_ref[g, 1, :, pl.ds(lane, LANES)] = imag[g * own : (g + 1) * own].astype(BF16)
        return carry

    lax.fori_loop(0, length // LANES, body, 0)


def mix(sums, weights, table, groups):
    _, channels, outs, length = weights.shape
    return pl.pallas_call(
        functools.partial(mix_kernel, groups),
        out_shape=jax.ShapeDtypeStruct((groups, 2, outs // groups, length), BF16),
        in_specs=[resident(), anywhere(), resident()],
        scratch_shapes=[
            pltpu.VMEM(sums.shape[1:], BF16),
            pltpu.VMEM(weights.shape, BF16),
            pltpu.SemaphoreType.DMA((length // LANES,)),
        ],
        compiler_params=pltpu.CompilerParams(vmem_limit_bytes=SMALL),
        cost_estimate=pl.CostEstimate(
            flops=4 * weights.size, bytes_accessed=2 * weights.size, transcendentals=0
        ),
        name="mix",
    )(sums, weights, table)


def compress_kernel(a_ref, b_ref, et_ref, o_ref):
    width = SLOTS * KZ
    mask = depth_mask(width)
    lane = lax.broadcasted_iota(jnp.int32, (1, 1, width), 2)
    twice = jnp.where(lane % KZ == 0, 1.0, 2.0).astype(F32)
    for k in range(a_ref.shape[-1] // width):
        lanes = slice(k * width, (k + 1) * width)
        total = a_ref[:, :, lanes].astype(F32) + b_ref[:, :, lanes].astype(F32)
        out = gather_depth(total * twice, et_ref[...], mask)
        o_ref[:, k * SLOTS : (k + 1) * SLOTS] = out.astype(BF16)


def compress(kept, got, table_t):
    _, channels, length = kept.shape
    return pl.pallas_call(
        compress_kernel,
        out_shape=jax.ShapeDtypeStruct((2 * KZ * channels, length // KZ), BF16),
        compiler_params=pltpu.CompilerParams(vmem_limit_bytes=SMALL),
        name="compress",
    )(kept, got, table_t)


def unmix_kernel(s_ref, w_hbm, e_ref, et_ref, o_ref, adj_ref, w_ref, sems):
    channels, outs, length = w_ref.shape[1:]
    for k in range(length // LANES):
        fetch_lanes(w_hbm, w_ref, sems, k).start()
    groups = s_ref.shape[0]
    mask = depth_mask(LANES)
    per = SLOTS * KZ // LANES
    wide = depth_mask(SLOTS * KZ)

    def chunk(k, carry):
        def body(j, inner):
            slot = pl.multiple_of(k * SLOTS, SLOTS)
            part = pl.multiple_of(j * LANES, LANES)
            lane = pl.multiple_of(k * SLOTS * KZ + j * LANES, LANES)
            fetch_lanes(w_hbm, w_ref, sems, k * per + j).wait()
            table = e_ref[:, pl.ds(part, LANES)]
            pieces = [spread(s_ref[g, :, pl.ds(slot, SLOTS)], table, mask, outs // groups) for g in range(groups)]
            gr = jnp.concatenate([piece[0] for piece in pieces], 0)
            gi = jnp.concatenate([piece[1] for piece in pieces], 0)
            for c in range(channels):
                w0 = w_ref[0, c, :, pl.ds(lane, LANES)].astype(F32)
                w1 = w_ref[1, c, :, pl.ds(lane, LANES)].astype(F32)
                adj_ref[0, c : c + 1, pl.ds(part, LANES)] = jnp.sum(w0 * gr + w1 * gi, axis=0, keepdims=True)
                adj_ref[1, c : c + 1, pl.ds(part, LANES)] = jnp.sum(w0 * gi - w1 * gr, axis=0, keepdims=True)
            return inner

        lax.fori_loop(0, per, body, 0)
        out = gather_depth(adj_ref[...], et_ref[...], wide)
        o_ref[:, pl.ds(pl.multiple_of(k * SLOTS, SLOTS), SLOTS)] = out.astype(BF16)
        return carry

    lax.fori_loop(0, length // (SLOTS * KZ), chunk, 0)


def unmix(sums, weights, table, table_t):
    _, channels, outs, length = weights.shape
    return pl.pallas_call(
        unmix_kernel,
        out_shape=jax.ShapeDtypeStruct((2 * KZ * channels, length // KZ), BF16),
        in_specs=[resident(), anywhere(), resident(), resident()],
        scratch_shapes=[
            pltpu.VMEM((2, channels, SLOTS * KZ), F32),
            pltpu.VMEM(weights.shape, BF16),
            pltpu.SemaphoreType.DMA((length // LANES,)),
        ],
        compiler_params=pltpu.CompilerParams(vmem_limit_bytes=SMALL),
        cost_estimate=pl.CostEstimate(
            flops=4 * weights.size, bytes_accessed=2 * weights.size, transcendentals=0
        ),
        name="unmix",
    )(sums, weights, table, table_t)


def bits_of(count):
    return tuple(1 << k for k in reversed(range(count.bit_length() - 1)))


def offsets(route):
    found = [0]
    for bit in route:
        found = found + [k ^ bit for k in found]
    return found


def exchange(value, axis, offset):
    size = lax.axis_size(axis)
    return lax.ppermute(value, axis, [(k, k ^ offset) for k in range(size)])


def per_device(field, forcing, slot_column, w_spec, skip_gain, bias):
    channels, planes, grid_len, _ = field.shape
    slabs, capacity = slot_column.shape
    groups = lax.axis_size("chan")
    own_rows = forcing.shape[1]
    factor = float(grid_len) ** -1.5

    row_np, col_np = plane_tables(grid_len)
    depth_np = depth_tables(planes, grid_len)
    rt = jnp.asarray(half_width(row_np))
    bd = jnp.asarray(half_width(np.swapaxes(row_np, 1, 2)) * ml_dtypes.bfloat16(factor))
    tx = jnp.asarray(half_width(col_np))
    txt = jnp.asarray(half_width(col_np.T))
    tz = jnp.asarray(half_width(depth_np))
    ts = jnp.asarray(half_width(np.swapaxes(depth_np, 1, 2)))
    table = jnp.asarray(half_width(spread_table()))
    table_t = jnp.asarray(half_width(spread_table().T))
    first = np.arange(slabs)[:, None] * planes * np.arange(KZ)[None, :] % grid_len
    first = np.repeat(first * (2.0 * math.pi / grid_len), KXY, axis=1)
    phases = jnp.asarray(np.stack([np.cos(first), np.sin(first)], 1).astype(np.float32))
    phase = lax.dynamic_index_in_dim(phases, lax.axis_index("slab"), 0, keepdims=False)

    slots = slot_column[:, None, :]
    me_slab, me_chan = lax.axis_index("slab"), lax.axis_index("chan")
    slab_bits = bits_of(slabs)
    routes = (slab_bits, slab_bits[-1:] + slab_bits[:-1])
    orders = [offsets(route) for route in routes]
    places = tuple(orders[1].index(offset) for offset in orders[0])
    gathered_slots = jnp.take(slots, me_slab ^ np.array(orders[0]), axis=0)

    forced_parts = [forcing]
    for bit in bits_of(groups):
        forced_parts += [exchange(part, "chan", bit) for part in forced_parts]
    forced_places = (me_chan ^ np.array(offsets(bits_of(groups)))).astype(jnp.int32)

    def send_sums(coefs, others):
        by_slot = to_slots(slots, coefs, others)
        return lax.all_to_all(by_slot, "slab", split_axis=0, concat_axis=0, tiled=True)

    def spread_spectra(own):
        pieces = [piece[None] for piece in jnp.split(own, 2, axis=0)]
        for step in range(len(slab_bits)):
            got = [exchange(piece, "slab", route[step]) for piece, route in zip(pieces, routes)]
            if step < len(slab_bits) - 1:
                pieces = [jnp.concatenate(pair, 0) for pair in zip(pieces, got)]
        return to_columns(gathered_slots, [pieces[0], got[0], pieces[1], got[1]], places, channels)

    tx_own = lax.dynamic_slice_in_dim(tx, lax.axis_index("chan") * own_rows, own_rows, 1)
    forced = analyse_forced(forcing, rt, tx_own, tz, phase, factor)
    others = [exchange(forced, "chan", k) for k in range(1, groups)]
    coefs = analyse(field, rt, tx, tz, phase, factor)
    sums = send_sums(coefs, [forced] + others)
    partial = mix(sums, w_spec, table, groups)
    for bit in reversed(bits_of(groups)):
        pairs = partial.reshape((partial.shape[0] // 2, 2) + partial.shape[1:])
        side = (me_chan // bit) % 2
        mine = lax.dynamic_index_in_dim(pairs, side, 1, keepdims=False)
        got = exchange(lax.dynamic_index_in_dim(pairs, 1 - side, 1, keepdims=False), "chan", bit)
        if mine.shape[0] > 1:
            partial = (mine.astype(F32) + got.astype(F32)).astype(BF16)
    spectra = spread_spectra(compress(mine[0], got[0], table_t))

    gain_rows = jnp.repeat(skip_gain, KXY)[:, None]
    centre = np.zeros((KXY, 2, ZB, KXY), np.float32)
    centre[KXY // 2, 0, :, KXY // 2] = 1.0 / factor
    centre = jnp.asarray(np.tile(centre.reshape(KXY, 2 * HALF), (channels, 1)))
    shift = centre * jnp.repeat(bias / skip_gain, KXY)[:, None]
    coefs_gelu = jnp.stack(
        [skip_gain**3 * (C1 * C2), skip_gain * C1, skip_gain * 0.5, skip_gain**2 * (6.0 * C1 * C2)], 1
    )
    output, grads, back = middle(
        spectra, field, forced_parts, forced_places, coefs_gelu, 1.0 / gain_rows, shift, rt, bd, tx, txt, tz, ts, phase, 0.5 * factor
    )
    doubling = jnp.where(jnp.arange(KZ) == 0, 1.0, 2.0).astype(F32)
    doubling = jnp.tile(jnp.repeat(doubling, channels), 2)[:, None]
    sums = jnp.sum(send_sums(back, []).astype(F32), axis=0)
    sums = (sums * doubling).astype(BF16)
    everyone = lax.all_gather(sums, "chan", axis=0)
    adjoint = spread_spectra(unmix(everyone, w_spec, table, table_t))
    gradient = finish(adjoint, grads, skip_gain * 0.5, bd, txt, ts, phase)
    return output, gradient


def solution(mesh):
    placed = (
        P("chan", "slab", None, None),
        P("slab", "chan", None),
        P(),
        P(None, "chan", None, "slab"),
        P("chan"),
        P("chan"),
    )
    return jax.shard_map(
        per_device,
        mesh=mesh,
        in_specs=placed,
        out_specs=(P("chan", "slab", None, None), P("chan", "slab", None, None)),
        check_vma=False,
    )
```

```python
import functools
import math

import jax
import jax.numpy as jnp
import ml_dtypes
import numpy as np
from jax import lax
from jax.experimental import pallas as pl
from jax.experimental.pallas import tpu as pltpu
from jax.sharding import PartitionSpec as P

KXY = 32
KZ = 16
ZB = 4
HALF = ZB * KXY
C1 = math.sqrt(2.0 / math.pi)
C2 = 0.044715
F32 = jnp.float32
BF16 = jnp.bfloat16
SLOTS = 128
SMALL = 16 * 2**20
LARGE = 54 * 2**20
AHEAD = 2


def dot(a, b):
    return jnp.dot(a, b, preferred_element_type=F32)


def angles(freqs, count, grid_len):
    turns = (freqs[:, None] * np.arange(count)[None, :]) % grid_len
    return turns * (2.0 * math.pi / grid_len)


def half_width(table):
    return table.astype(ml_dtypes.bfloat16)


def plane_tables(grid_len):
    angle = angles(np.arange(KXY) - KXY // 2, grid_len, grid_len)
    cosine, sine = np.cos(angle), np.sin(angle)
    rows = np.zeros((ZB, grid_len, 2, ZB, KXY))
    for i in range(ZB):
        rows[i, :, 0, i, :] = cosine.T
        rows[i, :, 1, i, :] = -sine.T
    rows = rows.reshape(ZB, grid_len, 2 * HALF)
    return rows, np.concatenate([cosine, sine], 0)


def depth_tables(planes, grid_len):
    angle = angles(np.arange(KZ), planes, grid_len)
    cosine, sine = np.cos(angle), np.sin(angle)
    table = np.zeros((planes // ZB, 2, ZB, KXY, 2, KZ, KXY))
    for b in range(planes // ZB):
        for i in range(ZB):
            for j in range(KXY):
                table[b, 0, i, j, 0, :, j] = cosine[:, b * ZB + i]
                table[b, 1, i, j, 0, :, j] = sine[:, b * ZB + i]
                table[b, 0, i, j, 1, :, j] = -sine[:, b * ZB + i]
                table[b, 1, i, j, 1, :, j] = cosine[:, b * ZB + i]
    return table.reshape(planes // ZB, 2 * HALF, 2 * KZ * KXY)


def spread_table():
    return np.repeat(np.eye(SLOTS), KZ, axis=1)


def whole(array):
    return pl.BlockSpec(array.shape, lambda *_: (0,) * len(array.shape))


def scalars():
    return pl.BlockSpec(memory_space=pltpu.SMEM)


def column_sums(u_ref, rt_ref, p_ref, first, last):
    rows = slice(first * 2 * KXY, last * 2 * KXY)
    total = dot(u_ref[0, rows], rt_ref[0])
    for i in range(1, ZB):
        total += dot(u_ref[i, rows], rt_ref[i])
    total = total.reshape(last - first, 2 * KXY, 2 * HALF)
    low, high = total[:, :KXY], total[:, KXY:]
    real = low[:, :, :HALF] + high[:, :, HALF:]
    imag = low[:, :, HALF:] - high[:, :, :HALF]
    rows = slice(first * KXY, last * KXY)
    p_ref[rows, :HALF] = real.reshape(-1, HALF).astype(BF16)
    p_ref[rows, HALF:] = imag.reshape(-1, HALF).astype(BF16)


def store_turned(total, ph_ref, out_ref, factor):
    half = KZ * KXY
    cosine, sine = ph_ref[0:1, :], ph_ref[1:2, :]
    real, imag = total[:, :half], total[:, half:]
    out_ref[:, :half] = ((real * cosine + imag * sine) * factor).astype(BF16)
    out_ref[:, half:] = ((imag * cosine - real * sine) * factor).astype(BF16)


def turn_spectra(q_ref, ph_ref, turned_ref):
    half = KZ * KXY
    cosine, sine = ph_ref[0:1, :], ph_ref[1:2, :]
    real, imag = q_ref[:, :half].astype(F32), q_ref[:, half:].astype(F32)
    turned_ref[:, :half] = (real * cosine - imag * sine).astype(BF16)
    turned_ref[:, half:] = (real * sine + imag * cosine).astype(BF16)


def resident():
    return pl.BlockSpec(memory_space=pltpu.VMEM)


def anywhere():
    return pl.BlockSpec(memory_space=pltpu.HBM)


def column_fields(zz_ref, txt, c):
    low = zz_ref[c * KXY : (c + 1) * KXY, :]
    high = jnp.concatenate([-low[:, HALF:], low[:, :HALF]], 1)
    return dot(txt, jnp.concatenate([low, high], 0)).astype(BF16)


def plane_rows(u_ref, tx, c, i, plane):
    u_ref[i, c * 2 * KXY : (c + 1) * 2 * KXY, :] = dot(tx, plane).astype(BF16)


def fetch_block(v_ref, kept_ref, sems, b):
    slot = lax.rem(b, kept_ref.shape[0])
    return pltpu.make_async_copy(v_ref.at[:, pl.ds(b * ZB, ZB)], kept_ref.at[slot], sems.at[slot])


def fetch_table(hbm_ref, table_ref, sems, b):
    slot = lax.rem(b, table_ref.shape[0])
    return pltpu.make_async_copy(hbm_ref.at[b], table_ref.at[slot], sems.at[slot])


def analyse_kernel(
    factor, v_ref, rt_ref, tx_ref, tz_hbm, ph_ref, out_ref, acc_ref, p_ref, u_ref, kept_ref, tz_ref, sems, tz_sems
):
    channels, planes = v_ref.shape[:2]
    blocks = planes // ZB
    half = channels // 2
    ahead = kept_ref.shape[0] - 1
    for b in range(ahead):
        fetch_block(v_ref, kept_ref, sems, b).start()
        fetch_table(tz_hbm, tz_ref, tz_sems, b).start()
    tx = tx_ref[...]
    acc_ref[...] = jnp.zeros_like(acc_ref)

    def body(b, carry):
        @pl.when(b + ahead < blocks)
        def _():
            fetch_block(v_ref, kept_ref, sems, b + ahead).start()
            fetch_table(tz_hbm, tz_ref, tz_sems, b + ahead).start()

        fetch_block(v_ref, kept_ref, sems, b).wait()
        slot = lax.rem(b, ahead + 1)
        for c in range(channels):
            for i in range(ZB):
                plane_rows(u_ref, tx, c, i, kept_ref[slot, c, i])
            if c == channels - 2:
                column_sums(u_ref, rt_ref, p_ref, 0, half)
        column_sums(u_ref, rt_ref, p_ref, half, channels)
        fetch_table(tz_hbm, tz_ref, tz_sems, b).wait()
        acc_ref[...] += dot(p_ref[...], tz_ref[slot])
        return carry

    lax.fori_loop(0, blocks, body, 0)
    store_turned(acc_ref[...], ph_ref, out_ref, factor)


def analyse(volume, rt, tx, tz, phase, factor):
    channels, planes, rows, grid_len = volume.shape
    width = 2 * KZ * KXY
    return pl.pallas_call(
        functools.partial(analyse_kernel, factor),
        in_specs=[anywhere(), resident(), resident(), anywhere(), resident()],
        out_specs=resident(),
        out_shape=jax.ShapeDtypeStruct((channels * KXY, width), BF16),
        scratch_shapes=[
            pltpu.VMEM((channels * KXY, width), F32),
            pltpu.VMEM((channels * KXY, 2 * HALF), BF16),
            pltpu.VMEM((ZB, channels * 2 * KXY, grid_len), BF16),
            pltpu.VMEM((3, channels, ZB, rows, grid_len), BF16),
            pltpu.VMEM((3,) + tz.shape[1:], BF16),
            pltpu.SemaphoreType.DMA((3,)),
            pltpu.SemaphoreType.DMA((3,)),
        ],
        compiler_params=pltpu.CompilerParams(vmem_limit_bytes=LARGE),
        cost_estimate=pl.CostEstimate(
            flops=8 * volume.size, bytes_accessed=volume.size // 8, transcendentals=0
        ),
        name="analyse",
    )(volume, rt, tx, tz, phase)


def forced_kernel(factor, v_ref, rt_ref, tx_ref, tz_hbm, ph_ref, out_ref, p_ref, u_ref, tz_ref, sem):
    tx = tx_ref[...]
    copy = pltpu.make_async_copy(tz_hbm, tz_ref, sem)
    copy.start()
    blocks = v_ref.shape[0] // ZB
    for b in range(blocks):
        for i in range(ZB):
            plane_rows(u_ref, tx, b, i, v_ref[b * ZB + i])
    column_sums(u_ref, rt_ref, p_ref, 0, blocks)
    copy.wait()
    total = dot(p_ref[:KXY], tz_ref[0])
    for b in range(1, blocks):
        total += dot(p_ref[b * KXY : (b + 1) * KXY], tz_ref[b])
    store_turned(total, ph_ref, out_ref, factor)


def analyse_forced(forcing, rt, tx, tz, phase, factor):
    planes, _, grid_len = forcing.shape
    blocks = planes // ZB
    return pl.pallas_call(
        functools.partial(forced_kernel, factor),
        in_specs=[resident(), resident(), resident(), anywhere(), resident()],
        out_shape=jax.ShapeDtypeStruct((KXY, 2 * KZ * KXY), BF16),
        scratch_shapes=[
            pltpu.VMEM((blocks * KXY, 2 * HALF), BF16),
            pltpu.VMEM((ZB, blocks * 2 * KXY, grid_len), BF16),
            pltpu.VMEM(tz.shape, BF16),
            pltpu.SemaphoreType.DMA,
        ],
        compiler_params=pltpu.CompilerParams(vmem_limit_bytes=SMALL),
        name="forced",
    )(forcing, rt, tx, tz, phase)


def gelu_planes(field, coefs_ref, c):
    cubic, linear, half, square = (coefs_ref[c, k].astype(BF16) for k in range(4))
    squared = field * field
    inner = field * (squared * cubic + linear)
    tangent = jnp.tanh(inner.astype(F32))
    upper = (1.0 + tangent).astype(BF16)
    lower = (1.0 - tangent).astype(BF16)
    value = field * (upper * half)
    slope = upper + value * lower * (squared * square + BF16(2.0 * C1))
    return value, value * slope


def send_block(buf_ref, o_ref, sems, b):
    slot = lax.rem(b, 2)
    return pltpu.make_async_copy(buf_ref.at[slot], o_ref.at[:, pl.ds(b * ZB, ZB)], sems.at[slot])


def send_half(buf_ref, o_ref, sems, b, h):
    slot = lax.rem(b, 2)
    half = buf_ref.shape[1] // 2
    part = pl.ds(h * half, half)
    return pltpu.make_async_copy(buf_ref.at[slot, part], o_ref.at[part, pl.ds(b * ZB, ZB)], sems.at[slot, h])


def fetch_forced(f_refs, raw_ref, sems, b, slot):
    return [
        pltpu.make_async_copy(ref.at[pl.ds(b * ZB, ZB)], raw_ref.at[slot, k], sems.at[slot, k])
        for k, ref in enumerate(f_refs)
    ]


def middle_kernel(factor, parts, *refs):
    q_ref, v_ref = refs[:2]
    f_refs = refs[2 : 2 + parts]
    (place_ref, coefs_ref, scale_ref, shift_ref, rt_ref, bd_ref, tx_ref, txt_ref, tz_hbm, ts_hbm, ph_ref) = refs[
        2 + parts : 13 + parts
    ]
    (o_ref, g_ref, back_ref, acc_ref, p_ref, u_ref, zz_ref, turned_ref, x_ref, f_ref, even_ref, odd_ref) = refs[
        13 + parts : 25 + parts
    ]
    kept_ref, buf_ref, grad_ref, raw_ref, tz_ref, ts_ref = refs[25 + parts : 31 + parts]
    out_sems, grad_sems, in_sems, v_sems, tz_sems, ts_sems = refs[31 + parts :]
    channels, planes = v_ref.shape[:2]
    blocks = planes // ZB
    half = channels // 2
    rows = raw_ref.shape[3]
    for copy in fetch_forced(f_refs, raw_ref, in_sems, 0, 0):
        copy.start()
    fetch_table(ts_hbm, ts_ref, ts_sems, 0).start()
    fetch_block(v_ref, kept_ref, v_sems, 0).start()
    fetch_table(tz_hbm, tz_ref, tz_sems, 0).start()
    turn_spectra(q_ref, ph_ref, turned_ref)
    acc_ref[...] = jnp.zeros_like(acc_ref)
    tx, txt = tx_ref[...], txt_ref[...]
    grads = (even_ref, odd_ref)

    def spatial(c, i):
        return dot(x_ref[c], bd_ref[i]).astype(BF16)

    def body(b, carry):
        slot = lax.rem(b, 2)

        @pl.when(b + 1 < blocks)
        def _():
            for copy in fetch_forced(f_refs, raw_ref, in_sems, b + 1, 1 - slot):
                copy.start()
            fetch_table(ts_hbm, ts_ref, ts_sems, b + 1).start()
            fetch_block(v_ref, kept_ref, v_sems, b + 1).start()
            fetch_table(tz_hbm, tz_ref, tz_sems, b + 1).start()

        for copy in fetch_forced(f_refs, raw_ref, in_sems, b, slot):
            copy.wait()
        fetch_table(ts_hbm, ts_ref, ts_sems, b).wait()
        fetch_block(v_ref, kept_ref, v_sems, b).wait()
        fetch_table(tz_hbm, tz_ref, tz_sems, b).wait()

        @pl.when(b > 1)
        def _():
            send_block(buf_ref, o_ref, out_sems, b - 2).wait()
            send_block(grad_ref, g_ref, grad_sems, b - 2).wait()

        for k in range(parts):
            f_ref[:, pl.ds(pl.multiple_of(place_ref[k] * rows, rows), rows), :] = raw_ref[slot, k]
        zz_ref[...] = (dot(turned_ref[...], ts_ref[slot]) * scale_ref[...] + shift_ref[...]).astype(BF16)
        for c in range(channels):
            x_ref[c] = column_fields(zz_ref, txt, c)
        for c in range(channels):
            ahead = spatial(c, 0)
            for i in range(ZB):
                here = ahead
                if i < ZB - 1:
                    ahead = spatial(c, i + 1)
                if c > 0:
                    plane_rows(u_ref, tx, c - 1, i, grads[(c - 1) % 2][i])
                value, grad = gelu_planes(here + (kept_ref[slot, c, i] + f_ref[i]), coefs_ref, c)
                buf_ref[slot, c, i] = value
                grad_ref[slot, c, i] = grad
                grads[c % 2][i] = grad
            if c == channels - 1:
                column_sums(u_ref, rt_ref, p_ref, 0, half)
        for i in range(ZB):
            plane_rows(u_ref, tx, channels - 1, i, grads[(channels - 1) % 2][i])
        column_sums(u_ref, rt_ref, p_ref, half, channels)
        acc_ref[...] += dot(p_ref[...], tz_ref[slot])
        send_block(buf_ref, o_ref, out_sems, b).start()
        send_block(grad_ref, g_ref, grad_sems, b).start()
        return carry

    lax.fori_loop(0, blocks, body, 0)
    store_turned(acc_ref[...], ph_ref, back_ref, factor)
    for b in (blocks - 2, blocks - 1):
        send_block(buf_ref, o_ref, out_sems, b).wait()
        send_block(grad_ref, g_ref, grad_sems, b).wait()


def middle(spectra, kept, forced, place, coefs, scale, shift, rt, bd, tx, txt, tz, ts, phase, factor):
    channels, planes, rows, grid_len = kept.shape
    width = 2 * KZ * KXY
    parts = len(forced)
    return pl.pallas_call(
        functools.partial(middle_kernel, factor, parts),
        in_specs=[resident(), anywhere()] + [anywhere()] * parts + [scalars()] * 2 + [resident()] * 6 + [anywhere()] * 2 + [resident()],
        out_specs=[anywhere(), anywhere(), resident()],
        out_shape=[
            jax.ShapeDtypeStruct(kept.shape, BF16),
            jax.ShapeDtypeStruct(kept.shape, BF16),
            jax.ShapeDtypeStruct((channels * KXY, width), BF16),
        ],
        scratch_shapes=[
            pltpu.VMEM((channels * KXY, width), F32),
            pltpu.VMEM((channels * KXY, 2 * HALF), BF16),
            pltpu.VMEM((ZB, channels * 2 * KXY, grid_len), BF16),
            pltpu.VMEM((channels * KXY, 2 * HALF), BF16),
            pltpu.VMEM((channels * KXY, width), BF16),
            pltpu.VMEM((channels, rows, 2 * HALF), BF16),
            pltpu.VMEM((ZB, rows, grid_len), BF16),
            pltpu.VMEM((ZB, rows, grid_len), BF16),
            pltpu.VMEM((ZB, rows, grid_len), BF16),
            pltpu.VMEM((2, channels, ZB, rows, grid_len), BF16),
            pltpu.VMEM((2, channels, ZB, rows, grid_len), BF16),
            pltpu.VMEM((2, channels, ZB, rows, grid_len), BF16),
            pltpu.VMEM((2, parts, ZB) + forced[0].shape[1:], BF16),
            pltpu.VMEM((2,) + tz.shape[1:], BF16),
            pltpu.VMEM((2,) + ts.shape[1:], BF16),
            pltpu.SemaphoreType.DMA((2,)),
            pltpu.SemaphoreType.DMA((2,)),
            pltpu.SemaphoreType.DMA((2, parts)),
            pltpu.SemaphoreType.DMA((2,)),
            pltpu.SemaphoreType.DMA((2,)),
            pltpu.SemaphoreType.DMA((2,)),
        ],
        compiler_params=pltpu.CompilerParams(vmem_limit_bytes=LARGE),
        cost_estimate=pl.CostEstimate(
            flops=1024 * kept.size, bytes_accessed=2 * kept.size, transcendentals=kept.size
        ),
        name="middle",
    )(spectra, kept, *forced, place, coefs, scale, shift, rt, bd, tx, txt, tz, ts, phase)


def finish_kernel(
    q_ref, g_ref, gain_ref, bd_ref, txt_ref, ts_hbm, ph_ref, o_ref, zz_ref, turned_ref, x_ref, kept_ref, buf_ref, ts_ref,
    sems, in_sems, ts_sems,
):
    channels, planes = g_ref.shape[:2]
    blocks = planes // ZB
    ahead = kept_ref.shape[0] - 1
    for b in range(ahead):
        fetch_table(ts_hbm, ts_ref, ts_sems, b).start()
        fetch_block(g_ref, kept_ref, in_sems, b).start()
    turn_spectra(q_ref, ph_ref, turned_ref)
    txt = txt_ref[...]

    def body(b, carry):
        @pl.when(b + ahead < blocks)
        def _():
            fetch_table(ts_hbm, ts_ref, ts_sems, b + ahead).start()
            fetch_block(g_ref, kept_ref, in_sems, b + ahead).start()

        slot = lax.rem(b, ahead + 1)
        fetch_table(ts_hbm, ts_ref, ts_sems, b).wait()
        fetch_block(g_ref, kept_ref, in_sems, b).wait()

        @pl.when(b > 1)
        def _():
            for h in range(2):
                send_half(buf_ref, o_ref, sems, b - 2, h).wait()

        zz_ref[...] = dot(turned_ref[...], ts_ref[slot]).astype(BF16)
        for c in range(channels):
            x_ref[c] = column_fields(zz_ref, txt, c)
        for c in range(channels):
            if c == channels // 2:
                send_half(buf_ref, o_ref, sems, b, 0).start()
            for i in range(ZB):
                plane = kept_ref[slot, c, i].astype(F32)
                buf_ref[lax.rem(b, 2), c, i] = (dot(x_ref[c], bd_ref[i]) + gain_ref[c] * plane).astype(BF16)
        send_half(buf_ref, o_ref, sems, b, 1).start()
        return carry

    lax.fori_loop(0, blocks, body, 0)
    for b in (blocks - 2, blocks - 1):
        for h in range(2):
            send_half(buf_ref, o_ref, sems, b, h).wait()


def finish(spectra, grads, gain, bd, txt, ts, phase):
    channels, planes, rows, grid_len = grads.shape
    width = 2 * KZ * KXY
    return pl.pallas_call(
        finish_kernel,
        in_specs=[resident(), anywhere(), scalars(), resident(), resident(), anywhere(), resident()],
        out_specs=anywhere(),
        out_shape=jax.ShapeDtypeStruct(grads.shape, BF16),
        scratch_shapes=[
            pltpu.VMEM((channels * KXY, 2 * HALF), BF16),
            pltpu.VMEM((channels * KXY, width), BF16),
            pltpu.VMEM((channels, rows, 2 * HALF), BF16),
            pltpu.VMEM((3, channels, ZB, rows, grid_len), BF16),
            pltpu.VMEM((2, channels, ZB, rows, grid_len), BF16),
            pltpu.VMEM((3,) + ts.shape[1:], BF16),
            pltpu.SemaphoreType.DMA((2, 2)),
            pltpu.SemaphoreType.DMA((3,)),
            pltpu.SemaphoreType.DMA((3,)),
        ],
        compiler_params=pltpu.CompilerParams(vmem_limit_bytes=LARGE),
        cost_estimate=pl.CostEstimate(
            flops=512 * grads.size, bytes_accessed=2 * grads.size, transcendentals=0
        ),
        name="finish",
    )(spectra, grads, gain, bd, txt, ts, phase)


def depth_mask(lanes):
    depth = lax.broadcasted_iota(jnp.int32, (KZ, 1, lanes), 0)
    lane = lax.broadcasted_iota(jnp.int32, (KZ, 1, lanes), 2)
    return (lane % KZ == depth).astype(F32)


def spread(sums, table, mask, channels):
    out = dot(sums, table)
    out = out.reshape(2, KZ, channels, out.shape[-1]) * mask[None]
    return jnp.sum(out, axis=1)


def gather_depth(values, table_t, mask):
    parts, channels, lanes = values.shape
    out = (values[:, None] * mask[None]).reshape(parts * KZ * channels, lanes)
    return dot(out.astype(BF16), table_t)


LANES = 512
GROUP = 8
WIDE = GROUP * KXY


def iota(shape, axis):
    return lax.broadcasted_iota(jnp.int32, shape, axis)


def one_hot(hit):
    return jnp.where(hit, 1.0, 0.0).astype(BF16)


def row_order(channels):
    shape = (WIDE, channels * KXY)
    row, lane = iota(shape, 0), iota(shape, 1)
    return one_hot((row // GROUP == lane % KXY) & (row % GROUP == lane // KXY))


def row_order_back(channels):
    shape = (channels * KXY, WIDE)
    row, lane = iota(shape, 0), iota(shape, 1)
    return one_hot((lane // GROUP == row % KXY) & (lane % GROUP == row // KXY))


def chosen(slots_ref, k, columns):
    capacity = slots_ref.shape[-1]
    return one_hot(iota((columns, capacity), 0) == slots_ref[k])


def own_lanes():
    shape = (GROUP, 1, WIDE)
    return (iota(shape, 0) == iota(shape, 2) // KXY).astype(F32)


def to_slots_kernel(places, unread, slots_ref, d_ref, *refs):
    others, a_refs, b_refs, t_ref = refs[: -5 - unread], refs[-5:-3], refs[-3:-1], refs[-1]
    channels = d_ref.shape[0] // KXY
    data = d_ref[...]
    if others:
        extra = others[0][...].astype(F32)
        for other in others[1:]:
            extra += other[...].astype(F32)
        data = data.astype(F32).reshape(channels, KXY, -1) + extra[None]
        data = data.reshape(channels * KXY, -1).astype(BF16)
    data = dot(row_order(channels), data).astype(BF16)
    row, lane = iota((WIDE, WIDE), 0), iota((WIDE, WIDE), 1)
    same = row % KXY == lane % KXY
    mask = own_lanes()
    groups = KXY // GROUP
    for m in range(GROUP):
        pick = one_hot(same & (row // KXY == m))
        for k in range(2 * KZ // GROUP):
            out = dot(data[:, k * WIDE : (k + 1) * WIDE], pick)
            out = jnp.sum(out.reshape(groups, GROUP, GROUP, WIDE) * mask[None], axis=1)
            first = (k * GROUP + m) * GROUP
            for g in range(groups):
                t_ref[first : first + GROUP, g * WIDE : (g + 1) * WIDE] = out[g]
    table = t_ref[...].astype(BF16)
    if channels < GROUP:
        shape = (2 * KZ * channels, WIDE)
        row, lane = iota(shape, 0), iota(shape, 1)
        keep = (row // channels == lane // GROUP) & (row % channels == lane % GROUP)
        table = dot(one_hot(keep), table).astype(BF16)
    half, rows = len(places) // 2, table.shape[0] // 2
    for k, place in enumerate(places):
        out = dot(table, chosen(slots_ref, k, KXY * KXY)).astype(BF16)
        a_refs[k // half][k % half] = out[:rows]
        b_refs[place // half][place % half] = out[rows:]


def to_slots(slots, coefs, others, places, after):
    slabs, _, capacity = slots.shape
    return pl.pallas_call(
        functools.partial(to_slots_kernel, places, len(after)),
        in_specs=[resident()] * (2 + len(others)) + [anywhere()] * len(after),
        out_shape=[jax.ShapeDtypeStruct((slabs // 2, coefs.shape[0] // 2, capacity), BF16)] * 4,
        scratch_shapes=[pltpu.VMEM((WIDE, KXY * KXY), F32)],
        compiler_params=pltpu.CompilerParams(vmem_limit_bytes=SMALL),
        name="to_slots",
    )(slots, coefs, *others, *after)


def to_columns_kernel(places, slots_ref, *refs):
    (a_refs, b_refs), (o_ref, t_ref) = (refs[:2], refs[2:4]), refs[4:]
    channels = o_ref.shape[0] // KXY
    columns = KXY * KXY
    half = slots_ref.shape[0] // 2

    def piece(pair, k):
        return pair[k // half][k % half]

    total = None
    for k, place in enumerate(places):
        both = jnp.concatenate([piece(a_refs, k), piece(b_refs, place)], 0)
        part = lax.dot_general(
            both, chosen(slots_ref, k, columns), (((1,), (1,)), ((), ())), preferred_element_type=F32
        )
        total = part if total is None else total + part
    if channels < GROUP:
        shape = (WIDE, 2 * KZ * channels)
        row, lane = iota(shape, 0), iota(shape, 1)
        keep = (lane // channels == row // GROUP) & (lane % channels == row % GROUP)
        total = dot(one_hot(keep), total.astype(BF16))
    t_ref[...] = total
    row, lane = iota((WIDE, WIDE), 0), iota((WIDE, WIDE), 1)
    same = row % KXY == lane % KXY
    mask = own_lanes()
    groups = KXY // GROUP
    back = row_order_back(channels)
    picks = [one_hot(same & (lane // KXY == m)) for m in range(GROUP)]
    for k in range(2 * KZ // GROUP):
        found = None
        for m in range(GROUP):
            first = (k * GROUP + m) * GROUP
            rows = t_ref[first : first + GROUP, :]
            parts = [(rows[None, :, g * WIDE : (g + 1) * WIDE] * mask).reshape(WIDE // groups, WIDE) for g in range(groups)]
            part = dot(jnp.concatenate(parts, 0).astype(BF16), picks[m])
            found = part if found is None else found + part
        o_ref[:, k * WIDE : (k + 1) * WIDE] = dot(back, found.astype(BF16)).astype(BF16)


def to_columns(slots, pieces, places, channels):
    return pl.pallas_call(
        functools.partial(to_columns_kernel, places),
        out_shape=jax.ShapeDtypeStruct((channels * KXY, 2 * KZ * KXY), BF16),
        scratch_shapes=[pltpu.VMEM((WIDE, KXY * KXY), F32)],
        compiler_params=pltpu.CompilerParams(vmem_limit_bytes=SMALL),
        name="to_columns",
    )(slots, *pieces)


def fetch_lanes(hbm_ref, w_ref, sems, k):
    lanes = pl.ds(k * LANES, LANES)
    return pltpu.make_async_copy(hbm_ref.at[:, :, :, lanes], w_ref.at[:, :, :, lanes], sems.at[k])


def fetch_ahead(w_hbm, w_ref, sems, k):
    chunks = w_ref.shape[-1] // LANES

    @pl.when(k + AHEAD < chunks)
    def _():
        fetch_lanes(w_hbm, w_ref, sems, k + AHEAD).start()

    fetch_lanes(w_hbm, w_ref, sems, k).wait()


def mix_kernel(groups, a_ref, b_ref, c_ref, d_ref, w_hbm, e_ref, o_ref, s_ref, w_ref, sems):
    channels, outs, length = w_ref.shape[1:]
    for k in range(min(AHEAD, length // LANES)):
        fetch_lanes(w_hbm, w_ref, sems, k).start()
    own = outs // groups
    mask = depth_mask(LANES)
    per = SLOTS * KZ // LANES
    rows = a_ref.shape[1]
    s_ref[:rows] = (a_ref[0].astype(F32) + b_ref[0].astype(F32)).astype(BF16)
    s_ref[rows:] = (c_ref[0].astype(F32) + d_ref[0].astype(F32)).astype(BF16)

    def body(k, carry):
        slot = pl.multiple_of(k // per * SLOTS, SLOTS)
        part = pl.multiple_of(k % per * LANES, LANES)
        lane = pl.multiple_of(k * LANES, LANES)
        fetch_ahead(w_hbm, w_ref, sems, k)
        u = spread(s_ref[:, pl.ds(slot, SLOTS)], e_ref[:, pl.ds(part, LANES)], mask, channels)
        real = jnp.zeros((outs, LANES), F32)
        imag = jnp.zeros((outs, LANES), F32)
        for c in range(channels):
            w0 = w_ref[0, c, :, pl.ds(lane, LANES)].astype(F32)
            w1 = w_ref[1, c, :, pl.ds(lane, LANES)].astype(F32)
            ur, ui = u[0, c : c + 1], u[1, c : c + 1]
            real += w0 * ur - w1 * ui
            imag += w1 * ur + w0 * ui
        for g in range(groups):
            o_ref[g, 0, :, pl.ds(lane, LANES)] = real[g * own : (g + 1) * own].astype(BF16)
            o_ref[g, 1, :, pl.ds(lane, LANES)] = imag[g * own : (g + 1) * own].astype(BF16)
        return carry

    lax.fori_loop(0, length // LANES, body, 0)


def mix(sums, weights, table, groups):
    _, channels, outs, length = weights.shape
    return pl.pallas_call(
        functools.partial(mix_kernel, groups),
        out_shape=jax.ShapeDtypeStruct((groups, 2, outs // groups, length), BF16),
        in_specs=[resident()] * 4 + [anywhere(), resident()],
        scratch_shapes=[
            pltpu.VMEM((2 * sums[0].shape[1], sums[0].shape[2]), BF16),
            pltpu.VMEM(weights.shape, BF16),
            pltpu.SemaphoreType.DMA((length // LANES,)),
        ],
        compiler_params=pltpu.CompilerParams(vmem_limit_bytes=SMALL),
        cost_estimate=pl.CostEstimate(
            flops=4 * weights.size, bytes_accessed=2 * weights.size, transcendentals=0
        ),
        name="mix",
    )(*sums, weights, table)


def compress_kernel(a_ref, b_ref, et_ref, o_ref):
    width = SLOTS * KZ
    mask = depth_mask(width)
    lane = lax.broadcasted_iota(jnp.int32, (1, 1, width), 2)
    twice = jnp.where(lane % KZ == 0, 1.0, 2.0).astype(F32)
    for k in range(a_ref.shape[-1] // width):
        lanes = slice(k * width, (k + 1) * width)
        total = a_ref[:, :, lanes].astype(F32) + b_ref[:, :, lanes].astype(F32)
        out = gather_depth(total * twice, et_ref[...], mask)
        o_ref[:, k * SLOTS : (k + 1) * SLOTS] = out.astype(BF16)


def compress(kept, got, table_t):
    _, channels, length = kept.shape
    return pl.pallas_call(
        compress_kernel,
        out_shape=jax.ShapeDtypeStruct((2 * KZ * channels, length // KZ), BF16),
        compiler_params=pltpu.CompilerParams(vmem_limit_bytes=SMALL),
        name="compress",
    )(kept, got, table_t)


def unmix_kernel(s_ref, w_hbm, e_ref, et_ref, o_ref, adj_ref, w_ref, sems):
    channels, outs, length = w_ref.shape[1:]
    for k in range(min(AHEAD, length // LANES)):
        fetch_lanes(w_hbm, w_ref, sems, k).start()
    groups = s_ref.shape[0]
    mask = depth_mask(LANES)
    per = SLOTS * KZ // LANES
    wide = depth_mask(SLOTS * KZ)

    def chunk(k, carry):
        def body(j, inner):
            slot = pl.multiple_of(k * SLOTS, SLOTS)
            part = pl.multiple_of(j * LANES, LANES)
            lane = pl.multiple_of(k * SLOTS * KZ + j * LANES, LANES)
            fetch_ahead(w_hbm, w_ref, sems, k * per + j)
            table = e_ref[:, pl.ds(part, LANES)]
            pieces = [spread(s_ref[g, :, pl.ds(slot, SLOTS)], table, mask, outs // groups) for g in range(groups)]
            gr = jnp.concatenate([piece[0] for piece in pieces], 0)
            gi = jnp.concatenate([piece[1] for piece in pieces], 0)
            for c in range(channels):
                w0 = w_ref[0, c, :, pl.ds(lane, LANES)].astype(F32)
                w1 = w_ref[1, c, :, pl.ds(lane, LANES)].astype(F32)
                adj_ref[0, c : c + 1, pl.ds(part, LANES)] = jnp.sum(w0 * gr + w1 * gi, axis=0, keepdims=True)
                adj_ref[1, c : c + 1, pl.ds(part, LANES)] = jnp.sum(w0 * gi - w1 * gr, axis=0, keepdims=True)
            return inner

        lax.fori_loop(0, per, body, 0)
        out = gather_depth(adj_ref[...], et_ref[...], wide)
        o_ref[:, pl.ds(pl.multiple_of(k * SLOTS, SLOTS), SLOTS)] = out.astype(BF16)
        return carry

    lax.fori_loop(0, length // (SLOTS * KZ), chunk, 0)


def unmix(sums, weights, table, table_t):
    _, channels, outs, length = weights.shape
    return pl.pallas_call(
        unmix_kernel,
        out_shape=jax.ShapeDtypeStruct((2 * KZ * channels, length // KZ), BF16),
        in_specs=[resident(), anywhere(), resident(), resident()],
        scratch_shapes=[
            pltpu.VMEM((2, channels, SLOTS * KZ), F32),
            pltpu.VMEM(weights.shape, BF16),
            pltpu.SemaphoreType.DMA((length // LANES,)),
        ],
        compiler_params=pltpu.CompilerParams(vmem_limit_bytes=SMALL),
        cost_estimate=pl.CostEstimate(
            flops=4 * weights.size, bytes_accessed=2 * weights.size, transcendentals=0
        ),
        name="unmix",
    )(sums, weights, table, table_t)


def bits_of(count):
    return tuple(1 << k for k in reversed(range(count.bit_length() - 1)))


def offsets(route):
    found = [0]
    for bit in route:
        found = found + [k ^ bit for k in found]
    return found


def exchange(value, axis, offset):
    size = lax.axis_size(axis)
    return lax.ppermute(value, axis, [(k, k ^ offset) for k in range(size)])


def per_device(field, forcing, slot_column, w_spec, skip_gain, bias):
    channels, planes, grid_len, _ = field.shape
    slabs, capacity = slot_column.shape
    groups = lax.axis_size("chan")
    own_rows = forcing.shape[1]
    factor = float(grid_len) ** -1.5

    row_np, col_np = plane_tables(grid_len)
    depth_np = depth_tables(planes, grid_len)
    rt = jnp.asarray(half_width(row_np))
    bd = jnp.asarray(half_width(np.swapaxes(row_np, 1, 2)) * ml_dtypes.bfloat16(factor))
    tx = jnp.asarray(half_width(col_np))
    txt = jnp.asarray(half_width(col_np.T))
    tz = jnp.asarray(half_width(depth_np))
    ts = jnp.asarray(half_width(np.swapaxes(depth_np, 1, 2)))
    table = jnp.asarray(half_width(spread_table()))
    table_t = jnp.asarray(half_width(spread_table().T))
    first = np.arange(slabs)[:, None] * planes * np.arange(KZ)[None, :] % grid_len
    first = np.repeat(first * (2.0 * math.pi / grid_len), KXY, axis=1)
    phases = jnp.asarray(np.stack([np.cos(first), np.sin(first)], 1).astype(np.float32))
    phase = lax.dynamic_index_in_dim(phases, lax.axis_index("slab"), 0, keepdims=False)

    slots = slot_column[:, None, :]
    me_slab, me_chan = lax.axis_index("slab"), lax.axis_index("chan")
    slab_bits = bits_of(slabs)
    routes = (slab_bits, slab_bits[-1:] + slab_bits[:-1])
    orders = [offsets(route) for route in routes]
    places = tuple(orders[1].index(offset) for offset in orders[0])
    gathered_slots = jnp.take(slots, me_slab ^ np.array(orders[0]), axis=0)

    forced_parts = [forcing]
    for bit in bits_of(groups):
        forced_parts += [exchange(part, "chan", bit) for part in forced_parts]
    forced_places = (me_chan ^ np.array(offsets(bits_of(groups)))).astype(jnp.int32)

    def send_sums(coefs, others, after):
        parts = to_slots(gathered_slots, coefs, others, places, after)
        kept, sent = [parts[0], parts[2]], [parts[1], parts[3]]
        for step in reversed(range(len(slab_bits))):
            got = [exchange(part, "slab", route[step]) for part, route in zip(sent, routes)]
            if step == 0:
                return kept[0], got[0], kept[1], got[1]
            sums = [(mine.astype(F32) + other.astype(F32)).astype(BF16) for mine, other in zip(kept, got)]
            kept, sent = zip(*[jnp.split(part, 2, axis=0) for part in sums])

    def spread_spectra(own):
        pieces = [piece[None] for piece in jnp.split(own, 2, axis=0)]
        for step in range(len(slab_bits)):
            got = [exchange(piece, "slab", route[step]) for piece, route in zip(pieces, routes)]
            if step < len(slab_bits) - 1:
                pieces = [jnp.concatenate(pair, 0) for pair in zip(pieces, got)]
        return to_columns(gathered_slots, [pieces[0], got[0], pieces[1], got[1]], places, channels)

    tx_own = lax.dynamic_slice_in_dim(tx, lax.axis_index("chan") * own_rows, own_rows, 1)
    forced = analyse_forced(forcing, rt, tx_own, tz, phase, factor)
    others = [exchange(forced, "chan", k) for k in range(1, groups)]
    coefs = analyse(field, rt, tx, tz, phase, factor)
    partial = mix(send_sums(coefs, [forced] + others, forced_parts[1:2]), w_spec, table, groups)
    for bit in reversed(bits_of(groups)):
        pairs = partial.reshape((partial.shape[0] // 2, 2) + partial.shape[1:])
        side = (me_chan // bit) % 2
        mine = lax.dynamic_index_in_dim(pairs, side, 1, keepdims=False)
        got = exchange(lax.dynamic_index_in_dim(pairs, 1 - side, 1, keepdims=False), "chan", bit)
        if mine.shape[0] > 1:
            partial = (mine.astype(F32) + got.astype(F32)).astype(BF16)
    spectra = spread_spectra(compress(mine[0], got[0], table_t))

    gain_rows = jnp.repeat(skip_gain, KXY)[:, None]
    centre = np.zeros((KXY, 2, ZB, KXY), np.float32)
    centre[KXY // 2, 0, :, KXY // 2] = 1.0 / factor
    centre = jnp.asarray(np.tile(centre.reshape(KXY, 2 * HALF), (channels, 1)))
    shift = centre * jnp.repeat(bias / skip_gain, KXY)[:, None]
    coefs_gelu = jnp.stack(
        [skip_gain**3 * (C1 * C2), skip_gain * C1, skip_gain * 0.5, skip_gain**2 * (6.0 * C1 * C2)], 1
    )
    output, grads, back = middle(
        spectra, field, forced_parts, forced_places, coefs_gelu, 1.0 / gain_rows, shift, rt, bd, tx, txt, tz, ts, phase, 0.5 * factor
    )
    doubling = jnp.where(jnp.arange(KZ) == 0, 1.0, 2.0).astype(F32)
    doubling = jnp.tile(jnp.repeat(doubling, channels), 2)[:, None]
    parts = [part[0].astype(F32) for part in send_sums(back, [], [])]
    sums = jnp.concatenate([parts[0] + parts[1], parts[2] + parts[3]], 0)
    sums = (sums * doubling).astype(BF16)
    everyone = lax.all_gather(sums, "chan", axis=0)
    adjoint = spread_spectra(unmix(everyone, w_spec, table, table_t))
    gradient = finish(adjoint, grads, skip_gain * 0.5, bd, txt, ts, phase)
    return output, gradient


def solution(mesh):
    placed = (
        P("chan", "slab", None, None),
        P("slab", "chan", None),
        P(),
        P(None, "chan", None, "slab"),
        P("chan"),
        P("chan"),
    )
    return jax.shard_map(
        per_device,
        mesh=mesh,
        in_specs=placed,
        out_specs=(P("chan", "slab", None, None), P("chan", "slab", None, None)),
        check_vma=False,
    )
```

```python
import functools
import math

import jax
import jax.numpy as jnp
import ml_dtypes
import numpy as np
from jax import lax
from jax.experimental import pallas as pl
from jax.experimental.pallas import tpu as pltpu
from jax.sharding import PartitionSpec as P

KXY = 32
KZ = 16
ZB = 4
HALF = ZB * KXY
C1 = math.sqrt(2.0 / math.pi)
C2 = 0.044715
F32 = jnp.float32
BF16 = jnp.bfloat16
SLOTS = 128
SMALL = 16 * 2**20
LARGE = 54 * 2**20
AHEAD = 2


def dot(a, b):
    return jnp.dot(a, b, preferred_element_type=F32)


def angles(freqs, count, grid_len):
    turns = (freqs[:, None] * np.arange(count)[None, :]) % grid_len
    return turns * (2.0 * math.pi / grid_len)


def half_width(table):
    return table.astype(ml_dtypes.bfloat16)


def plane_tables(grid_len):
    angle = angles(np.arange(KXY) - KXY // 2, grid_len, grid_len)
    cosine, sine = np.cos(angle), np.sin(angle)
    rows = np.zeros((ZB, grid_len, 2, ZB, KXY))
    for i in range(ZB):
        rows[i, :, 0, i, :] = cosine.T
        rows[i, :, 1, i, :] = -sine.T
    rows = rows.reshape(ZB, grid_len, 2 * HALF)
    return rows, np.concatenate([cosine, sine], 0)


def depth_tables(planes, grid_len):
    angle = angles(np.arange(KZ), planes, grid_len)
    cosine, sine = np.cos(angle), np.sin(angle)
    table = np.zeros((planes // ZB, 2, ZB, KXY, 2, KZ, KXY))
    for b in range(planes // ZB):
        for i in range(ZB):
            for j in range(KXY):
                table[b, 0, i, j, 0, :, j] = cosine[:, b * ZB + i]
                table[b, 1, i, j, 0, :, j] = sine[:, b * ZB + i]
                table[b, 0, i, j, 1, :, j] = -sine[:, b * ZB + i]
                table[b, 1, i, j, 1, :, j] = cosine[:, b * ZB + i]
    return table.reshape(planes // ZB, 2 * HALF, 2 * KZ * KXY)


def spread_table():
    return np.repeat(np.eye(SLOTS), KZ, axis=1)


def whole(array):
    return pl.BlockSpec(array.shape, lambda *_: (0,) * len(array.shape))


def scalars():
    return pl.BlockSpec(memory_space=pltpu.SMEM)


def column_sums(u_ref, rt_ref, p_ref, first, last):
    rows = slice(first * 2 * KXY, last * 2 * KXY)
    total = dot(u_ref[0, rows], rt_ref[0])
    for i in range(1, ZB):
        total += dot(u_ref[i, rows], rt_ref[i])
    total = total.reshape(last - first, 2 * KXY, 2 * HALF)
    low, high = total[:, :KXY], total[:, KXY:]
    real = low[:, :, :HALF] + high[:, :, HALF:]
    imag = low[:, :, HALF:] - high[:, :, :HALF]
    rows = slice(first * KXY, last * KXY)
    p_ref[rows, :HALF] = real.reshape(-1, HALF).astype(BF16)
    p_ref[rows, HALF:] = imag.reshape(-1, HALF).astype(BF16)


def store_turned(total, ph_ref, out_ref, factor):
    half = KZ * KXY
    cosine, sine = ph_ref[0:1, :], ph_ref[1:2, :]
    real, imag = total[:, :half], total[:, half:]
    out_ref[:, :half] = ((real * cosine + imag * sine) * factor).astype(BF16)
    out_ref[:, half:] = ((imag * cosine - real * sine) * factor).astype(BF16)


def turn_spectra(q_ref, ph_ref, turned_ref):
    half = KZ * KXY
    cosine, sine = ph_ref[0:1, :], ph_ref[1:2, :]
    real, imag = q_ref[:, :half].astype(F32), q_ref[:, half:].astype(F32)
    turned_ref[:, :half] = (real * cosine - imag * sine).astype(BF16)
    turned_ref[:, half:] = (real * sine + imag * cosine).astype(BF16)


def resident():
    return pl.BlockSpec(memory_space=pltpu.VMEM)


def anywhere():
    return pl.BlockSpec(memory_space=pltpu.HBM)


def column_fields(zz_ref, txt, c):
    low = zz_ref[c * KXY : (c + 1) * KXY, :]
    high = jnp.concatenate([-low[:, HALF:], low[:, :HALF]], 1)
    return dot(txt, jnp.concatenate([low, high], 0)).astype(BF16)


def plane_rows(u_ref, tx, c, i, plane):
    u_ref[i, c * 2 * KXY : (c + 1) * 2 * KXY, :] = dot(tx, plane).astype(BF16)


def fetch_block(v_ref, kept_ref, sems, b):
    slot = lax.rem(b, kept_ref.shape[0])
    return pltpu.make_async_copy(v_ref.at[:, pl.ds(b * ZB, ZB)], kept_ref.at[slot], sems.at[slot])


def fetch_table(hbm_ref, table_ref, sems, b):
    slot = lax.rem(b, table_ref.shape[0])
    return pltpu.make_async_copy(hbm_ref.at[b], table_ref.at[slot], sems.at[slot])


def analyse_kernel(
    factor, v_ref, rt_ref, tx_ref, tz_hbm, ph_ref, out_ref, acc_ref, p_ref, u_ref, kept_ref, tz_ref, sems, tz_sems
):
    channels, planes = v_ref.shape[:2]
    blocks = planes // ZB
    half = channels // 2
    ahead = kept_ref.shape[0] - 1
    for b in range(ahead):
        fetch_block(v_ref, kept_ref, sems, b).start()
        fetch_table(tz_hbm, tz_ref, tz_sems, b).start()
    tx = tx_ref[...]
    acc_ref[...] = jnp.zeros_like(acc_ref)

    def body(b, carry):
        @pl.when(b + ahead < blocks)
        def _():
            fetch_block(v_ref, kept_ref, sems, b + ahead).start()
            fetch_table(tz_hbm, tz_ref, tz_sems, b + ahead).start()

        fetch_block(v_ref, kept_ref, sems, b).wait()
        slot = lax.rem(b, ahead + 1)
        for c in range(channels):
            for i in range(ZB):
                plane_rows(u_ref, tx, c, i, kept_ref[slot, c, i])
            if c == channels - 2:
                column_sums(u_ref, rt_ref, p_ref, 0, half)
        column_sums(u_ref, rt_ref, p_ref, half, channels)
        fetch_table(tz_hbm, tz_ref, tz_sems, b).wait()
        acc_ref[...] += dot(p_ref[...], tz_ref[slot])
        return carry

    lax.fori_loop(0, blocks, body, 0)
    store_turned(acc_ref[...], ph_ref, out_ref, factor)


def analyse(volume, rt, tx, tz, phase, factor):
    channels, planes, rows, grid_len = volume.shape
    width = 2 * KZ * KXY
    return pl.pallas_call(
        functools.partial(analyse_kernel, factor),
        in_specs=[anywhere(), resident(), resident(), anywhere(), resident()],
        out_specs=resident(),
        out_shape=pltpu.VMEM((channels * KXY, width), BF16),
        scratch_shapes=[
            pltpu.VMEM((channels * KXY, width), F32),
            pltpu.VMEM((channels * KXY, 2 * HALF), BF16),
            pltpu.VMEM((ZB, channels * 2 * KXY, grid_len), BF16),
            pltpu.VMEM((3, channels, ZB, rows, grid_len), BF16),
            pltpu.VMEM((3,) + tz.shape[1:], BF16),
            pltpu.SemaphoreType.DMA((3,)),
            pltpu.SemaphoreType.DMA((3,)),
        ],
        compiler_params=pltpu.CompilerParams(vmem_limit_bytes=LARGE),
        cost_estimate=pl.CostEstimate(
            flops=8 * volume.size, bytes_accessed=volume.size // 8, transcendentals=0
        ),
        name="analyse",
    )(volume, rt, tx, tz, phase)


def forced_kernel(factor, v_ref, rt_ref, tx_ref, tz_hbm, ph_ref, out_ref, p_ref, u_ref, tz_ref, sem):
    tx = tx_ref[...]
    copy = pltpu.make_async_copy(tz_hbm, tz_ref, sem)
    copy.start()
    blocks = v_ref.shape[0] // ZB
    for b in range(blocks):
        for i in range(ZB):
            plane_rows(u_ref, tx, b, i, v_ref[b * ZB + i])
    column_sums(u_ref, rt_ref, p_ref, 0, blocks)
    copy.wait()
    total = dot(p_ref[:KXY], tz_ref[0])
    for b in range(1, blocks):
        total += dot(p_ref[b * KXY : (b + 1) * KXY], tz_ref[b])
    store_turned(total, ph_ref, out_ref, factor)


def analyse_forced(forcing, rt, tx, tz, phase, factor):
    planes, _, grid_len = forcing.shape
    blocks = planes // ZB
    return pl.pallas_call(
        functools.partial(forced_kernel, factor),
        in_specs=[resident(), resident(), resident(), anywhere(), resident()],
        out_shape=jax.ShapeDtypeStruct((KXY, 2 * KZ * KXY), BF16),
        scratch_shapes=[
            pltpu.VMEM((blocks * KXY, 2 * HALF), BF16),
            pltpu.VMEM((ZB, blocks * 2 * KXY, grid_len), BF16),
            pltpu.VMEM(tz.shape, BF16),
            pltpu.SemaphoreType.DMA,
        ],
        compiler_params=pltpu.CompilerParams(vmem_limit_bytes=LARGE),
        name="forced",
    )(forcing, rt, tx, tz, phase)


def gelu_planes(field, coefs_ref, c):
    cubic, linear, half, square = (coefs_ref[c, k].astype(BF16) for k in range(4))
    squared = field * field
    inner = field * (squared * cubic + linear)
    tangent = jnp.tanh(inner.astype(F32))
    upper = (1.0 + tangent).astype(BF16)
    lower = (1.0 - tangent).astype(BF16)
    value = field * (upper * half)
    slope = upper + value * lower * (squared * square + BF16(2.0 * C1))
    return value, value * slope


def send_block(buf_ref, o_ref, sems, b):
    slot = lax.rem(b, 2)
    return pltpu.make_async_copy(buf_ref.at[slot], o_ref.at[:, pl.ds(b * ZB, ZB)], sems.at[slot])


def send_half(buf_ref, o_ref, sems, b, h):
    slot = lax.rem(b, 2)
    half = buf_ref.shape[1] // 2
    part = pl.ds(h * half, half)
    return pltpu.make_async_copy(buf_ref.at[slot, part], o_ref.at[part, pl.ds(b * ZB, ZB)], sems.at[slot, h])


def fetch_forced(f_refs, raw_ref, sems, b, slot):
    return [
        pltpu.make_async_copy(ref.at[pl.ds(b * ZB, ZB)], raw_ref.at[slot, k], sems.at[slot, k])
        for k, ref in enumerate(f_refs)
    ]


def middle_kernel(factor, parts, *refs):
    q_ref, v_ref = refs[:2]
    f_refs = refs[2 : 2 + parts]
    (place_ref, coefs_ref, scale_ref, shift_ref, rt_ref, bd_ref, tx_ref, txt_ref, tz_hbm, ts_hbm, ph_ref) = refs[
        2 + parts : 13 + parts
    ]
    (o_ref, g_ref, back_ref, acc_ref, p_ref, u_ref, zz_ref, turned_ref, x_ref, f_ref, even_ref, odd_ref) = refs[
        13 + parts : 25 + parts
    ]
    kept_ref, buf_ref, grad_ref, raw_ref, tz_ref, ts_ref = refs[25 + parts : 31 + parts]
    out_sems, grad_sems, in_sems, v_sems, tz_sems, ts_sems = refs[31 + parts :]
    channels, planes = v_ref.shape[:2]
    blocks = planes // ZB
    half = channels // 2
    rows = raw_ref.shape[3]
    for copy in fetch_forced(f_refs, raw_ref, in_sems, 0, 0):
        copy.start()
    fetch_table(ts_hbm, ts_ref, ts_sems, 0).start()
    fetch_block(v_ref, kept_ref, v_sems, 0).start()
    fetch_table(tz_hbm, tz_ref, tz_sems, 0).start()
    turn_spectra(q_ref, ph_ref, turned_ref)
    acc_ref[...] = jnp.zeros_like(acc_ref)
    tx, txt = tx_ref[...], txt_ref[...]
    grads = (even_ref, odd_ref)

    def spatial(c, i):
        return dot(x_ref[c], bd_ref[i]).astype(BF16)

    def body(b, carry):
        slot = lax.rem(b, 2)

        @pl.when(b + 1 < blocks)
        def _():
            for copy in fetch_forced(f_refs, raw_ref, in_sems, b + 1, 1 - slot):
                copy.start()
            fetch_table(ts_hbm, ts_ref, ts_sems, b + 1).start()
            fetch_block(v_ref, kept_ref, v_sems, b + 1).start()
            fetch_table(tz_hbm, tz_ref, tz_sems, b + 1).start()

        for copy in fetch_forced(f_refs, raw_ref, in_sems, b, slot):
            copy.wait()
        fetch_table(ts_hbm, ts_ref, ts_sems, b).wait()
        fetch_block(v_ref, kept_ref, v_sems, b).wait()
        fetch_table(tz_hbm, tz_ref, tz_sems, b).wait()

        @pl.when(b > 1)
        def _():
            send_block(buf_ref, o_ref, out_sems, b - 2).wait()
            send_block(grad_ref, g_ref, grad_sems, b - 2).wait()

        for k in range(parts):
            f_ref[:, pl.ds(pl.multiple_of(place_ref[k] * rows, rows), rows), :] = raw_ref[slot, k]
        zz_ref[...] = (dot(turned_ref[...], ts_ref[slot]) * scale_ref[...] + shift_ref[...]).astype(BF16)
        for c in range(channels):
            x_ref[c] = column_fields(zz_ref, txt, c)
        for c in range(channels):
            ahead = spatial(c, 0)
            for i in range(ZB):
                here = ahead
                if i < ZB - 1:
                    ahead = spatial(c, i + 1)
                if c > 0:
                    plane_rows(u_ref, tx, c - 1, i, grads[(c - 1) % 2][i])
                value, grad = gelu_planes(here + (kept_ref[slot, c, i] + f_ref[i]), coefs_ref, c)
                buf_ref[slot, c, i] = value
                grad_ref[slot, c, i] = grad
                grads[c % 2][i] = grad
            if c == channels - 1:
                column_sums(u_ref, rt_ref, p_ref, 0, half)
        for i in range(ZB):
            plane_rows(u_ref, tx, channels - 1, i, grads[(channels - 1) % 2][i])
        column_sums(u_ref, rt_ref, p_ref, half, channels)
        acc_ref[...] += dot(p_ref[...], tz_ref[slot])
        send_block(buf_ref, o_ref, out_sems, b).start()
        send_block(grad_ref, g_ref, grad_sems, b).start()
        return carry

    lax.fori_loop(0, blocks, body, 0)
    store_turned(acc_ref[...], ph_ref, back_ref, factor)
    for b in (blocks - 2, blocks - 1):
        send_block(buf_ref, o_ref, out_sems, b).wait()
        send_block(grad_ref, g_ref, grad_sems, b).wait()


def middle(spectra, kept, forced, place, coefs, scale, shift, rt, bd, tx, txt, tz, ts, phase, factor):
    channels, planes, rows, grid_len = kept.shape
    width = 2 * KZ * KXY
    parts = len(forced)
    return pl.pallas_call(
        functools.partial(middle_kernel, factor, parts),
        in_specs=[resident(), anywhere()] + [anywhere()] * parts + [scalars()] * 2 + [resident()] * 6 + [anywhere()] * 2 + [resident()],
        out_specs=[anywhere(), anywhere(), resident()],
        out_shape=[
            jax.ShapeDtypeStruct(kept.shape, BF16),
            jax.ShapeDtypeStruct(kept.shape, BF16),
            pltpu.VMEM((channels * KXY, width), BF16),
        ],
        scratch_shapes=[
            pltpu.VMEM((channels * KXY, width), F32),
            pltpu.VMEM((channels * KXY, 2 * HALF), BF16),
            pltpu.VMEM((ZB, channels * 2 * KXY, grid_len), BF16),
            pltpu.VMEM((channels * KXY, 2 * HALF), BF16),
            pltpu.VMEM((channels * KXY, width), BF16),
            pltpu.VMEM((channels, rows, 2 * HALF), BF16),
            pltpu.VMEM((ZB, rows, grid_len), BF16),
            pltpu.VMEM((ZB, rows, grid_len), BF16),
            pltpu.VMEM((ZB, rows, grid_len), BF16),
            pltpu.VMEM((2, channels, ZB, rows, grid_len), BF16),
            pltpu.VMEM((2, channels, ZB, rows, grid_len), BF16),
            pltpu.VMEM((2, channels, ZB, rows, grid_len), BF16),
            pltpu.VMEM((2, parts, ZB) + forced[0].shape[1:], BF16),
            pltpu.VMEM((2,) + tz.shape[1:], BF16),
            pltpu.VMEM((2,) + ts.shape[1:], BF16),
            pltpu.SemaphoreType.DMA((2,)),
            pltpu.SemaphoreType.DMA((2,)),
            pltpu.SemaphoreType.DMA((2, parts)),
            pltpu.SemaphoreType.DMA((2,)),
            pltpu.SemaphoreType.DMA((2,)),
            pltpu.SemaphoreType.DMA((2,)),
        ],
        compiler_params=pltpu.CompilerParams(vmem_limit_bytes=LARGE),
        cost_estimate=pl.CostEstimate(
            flops=1024 * kept.size, bytes_accessed=2 * kept.size, transcendentals=kept.size
        ),
        name="middle",
    )(spectra, kept, *forced, place, coefs, scale, shift, rt, bd, tx, txt, tz, ts, phase)


def finish_kernel(
    q_ref, g_ref, gain_ref, bd_ref, txt_ref, ts_hbm, ph_ref, o_ref, zz_ref, turned_ref, x_ref, kept_ref, buf_ref, ts_ref,
    sems, in_sems, ts_sems,
):
    channels, planes = g_ref.shape[:2]
    blocks = planes // ZB
    ahead = kept_ref.shape[0] - 1
    for b in range(ahead):
        fetch_table(ts_hbm, ts_ref, ts_sems, b).start()
        fetch_block(g_ref, kept_ref, in_sems, b).start()
    turn_spectra(q_ref, ph_ref, turned_ref)
    txt = txt_ref[...]

    def body(b, carry):
        @pl.when(b + ahead < blocks)
        def _():
            fetch_table(ts_hbm, ts_ref, ts_sems, b + ahead).start()
            fetch_block(g_ref, kept_ref, in_sems, b + ahead).start()

        slot = lax.rem(b, ahead + 1)
        fetch_table(ts_hbm, ts_ref, ts_sems, b).wait()
        fetch_block(g_ref, kept_ref, in_sems, b).wait()

        @pl.when(b > 1)
        def _():
            for h in range(2):
                send_half(buf_ref, o_ref, sems, b - 2, h).wait()

        zz_ref[...] = dot(turned_ref[...], ts_ref[slot]).astype(BF16)
        for c in range(channels):
            x_ref[c] = column_fields(zz_ref, txt, c)
        for c in range(channels):
            if c == channels // 2:
                send_half(buf_ref, o_ref, sems, b, 0).start()
            for i in range(ZB):
                plane = kept_ref[slot, c, i].astype(F32)
                buf_ref[lax.rem(b, 2), c, i] = (dot(x_ref[c], bd_ref[i]) + gain_ref[c] * plane).astype(BF16)
        send_half(buf_ref, o_ref, sems, b, 1).start()
        return carry

    lax.fori_loop(0, blocks, body, 0)
    for b in (blocks - 2, blocks - 1):
        for h in range(2):
            send_half(buf_ref, o_ref, sems, b, h).wait()


def finish(spectra, grads, gain, bd, txt, ts, phase):
    channels, planes, rows, grid_len = grads.shape
    width = 2 * KZ * KXY
    return pl.pallas_call(
        finish_kernel,
        in_specs=[resident(), anywhere(), scalars(), resident(), resident(), anywhere(), resident()],
        out_specs=anywhere(),
        out_shape=jax.ShapeDtypeStruct(grads.shape, BF16),
        scratch_shapes=[
            pltpu.VMEM((channels * KXY, 2 * HALF), BF16),
            pltpu.VMEM((channels * KXY, width), BF16),
            pltpu.VMEM((channels, rows, 2 * HALF), BF16),
            pltpu.VMEM((3, channels, ZB, rows, grid_len), BF16),
            pltpu.VMEM((2, channels, ZB, rows, grid_len), BF16),
            pltpu.VMEM((3,) + ts.shape[1:], BF16),
            pltpu.SemaphoreType.DMA((2, 2)),
            pltpu.SemaphoreType.DMA((3,)),
            pltpu.SemaphoreType.DMA((3,)),
        ],
        compiler_params=pltpu.CompilerParams(vmem_limit_bytes=LARGE),
        cost_estimate=pl.CostEstimate(
            flops=512 * grads.size, bytes_accessed=2 * grads.size, transcendentals=0
        ),
        name="finish",
    )(spectra, grads, gain, bd, txt, ts, phase)


def depth_mask(lanes):
    depth = lax.broadcasted_iota(jnp.int32, (KZ, 1, lanes), 0)
    lane = lax.broadcasted_iota(jnp.int32, (KZ, 1, lanes), 2)
    return (lane % KZ == depth).astype(F32)


def spread(sums, table, mask, channels):
    out = dot(sums, table)
    out = out.reshape(2, KZ, channels, out.shape[-1]) * mask[None]
    return jnp.sum(out, axis=1)


def gather_depth(values, table_t, mask):
    parts, channels, lanes = values.shape
    out = (values[:, None] * mask[None]).reshape(parts * KZ * channels, lanes)
    return dot(out.astype(BF16), table_t)


LANES = 512
GROUP = 8
WIDE = GROUP * KXY


def iota(shape, axis):
    return lax.broadcasted_iota(jnp.int32, shape, axis)


def one_hot(hit):
    return jnp.where(hit, 1.0, 0.0).astype(BF16)


def row_order(channels):
    shape = (WIDE, channels * KXY)
    row, lane = iota(shape, 0), iota(shape, 1)
    return one_hot((row // GROUP == lane % KXY) & (row % GROUP == lane // KXY))


def row_order_back(channels):
    shape = (channels * KXY, WIDE)
    row, lane = iota(shape, 0), iota(shape, 1)
    return one_hot((lane // GROUP == row % KXY) & (lane % GROUP == row // KXY))


def chosen(slots_ref, k, columns):
    capacity = slots_ref.shape[-1]
    return one_hot(iota((columns, capacity), 0) == slots_ref[k])


def own_lanes():
    shape = (GROUP, 1, WIDE)
    return (iota(shape, 0) == iota(shape, 2) // KXY).astype(F32)


def to_slots_kernel(places, unread, slots_ref, d_ref, *refs):
    others, a_refs, b_refs, t_ref = refs[: -5 - unread], refs[-5:-3], refs[-3:-1], refs[-1]
    channels = d_ref.shape[0] // KXY
    data = d_ref[...]
    if others:
        extra = others[0][...].astype(F32)
        for other in others[1:]:
            extra += other[...].astype(F32)
        data = data.astype(F32).reshape(channels, KXY, -1) + extra[None]
        data = data.reshape(channels * KXY, -1).astype(BF16)
    data = dot(row_order(channels), data).astype(BF16)
    row, lane = iota((WIDE, WIDE), 0), iota((WIDE, WIDE), 1)
    same = row % KXY == lane % KXY
    mask = own_lanes()
    groups = KXY // GROUP
    for m in range(GROUP):
        pick = one_hot(same & (row // KXY == m))
        for k in range(2 * KZ // GROUP):
            out = dot(data[:, k * WIDE : (k + 1) * WIDE], pick)
            out = jnp.sum(out.reshape(groups, GROUP, GROUP, WIDE) * mask[None], axis=1)
            first = (k * GROUP + m) * GROUP
            for g in range(groups):
                t_ref[first : first + GROUP, g * WIDE : (g + 1) * WIDE] = out[g]
    table = t_ref[...].astype(BF16)
    if channels < GROUP:
        shape = (2 * KZ * channels, WIDE)
        row, lane = iota(shape, 0), iota(shape, 1)
        keep = (row // channels == lane // GROUP) & (row % channels == lane % GROUP)
        table = dot(one_hot(keep), table).astype(BF16)
    half, rows = len(places) // 2, table.shape[0] // 2
    for k, place in enumerate(places):
        out = dot(table, chosen(slots_ref, k, KXY * KXY)).astype(BF16)
        a_refs[k // half][k % half] = out[:rows]
        b_refs[place // half][place % half] = out[rows:]


def to_slots(slots, coefs, others, places, after):
    slabs, _, capacity = slots.shape
    return pl.pallas_call(
        functools.partial(to_slots_kernel, places, len(after)),
        in_specs=[resident()] * (2 + len(others)) + [anywhere()] * len(after),
        out_shape=[jax.ShapeDtypeStruct((slabs // 2, coefs.shape[0] // 2, capacity), BF16)] * 4,
        scratch_shapes=[pltpu.VMEM((WIDE, KXY * KXY), F32)],
        compiler_params=pltpu.CompilerParams(vmem_limit_bytes=SMALL),
        name="to_slots",
    )(slots, coefs, *others, *after)


def to_columns_kernel(places, slots_ref, *refs):
    (a_refs, b_refs), (o_ref, t_ref) = (refs[:2], refs[2:4]), refs[4:]
    channels = o_ref.shape[0] // KXY
    columns = KXY * KXY
    half = slots_ref.shape[0] // 2

    def piece(pair, k):
        return pair[k // half][k % half]

    total = None
    for k, place in enumerate(places):
        both = jnp.concatenate([piece(a_refs, k), piece(b_refs, place)], 0)
        part = lax.dot_general(
            both, chosen(slots_ref, k, columns), (((1,), (1,)), ((), ())), preferred_element_type=F32
        )
        total = part if total is None else total + part
    if channels < GROUP:
        shape = (WIDE, 2 * KZ * channels)
        row, lane = iota(shape, 0), iota(shape, 1)
        keep = (lane // channels == row // GROUP) & (lane % channels == row % GROUP)
        total = dot(one_hot(keep), total.astype(BF16))
    t_ref[...] = total
    row, lane = iota((WIDE, WIDE), 0), iota((WIDE, WIDE), 1)
    same = row % KXY == lane % KXY
    mask = own_lanes()
    groups = KXY // GROUP
    back = row_order_back(channels)
    picks = [one_hot(same & (lane // KXY == m)) for m in range(GROUP)]
    for k in range(2 * KZ // GROUP):
        found = None
        for m in range(GROUP):
            first = (k * GROUP + m) * GROUP
            rows = t_ref[first : first + GROUP, :]
            parts = [(rows[None, :, g * WIDE : (g + 1) * WIDE] * mask).reshape(WIDE // groups, WIDE) for g in range(groups)]
            part = dot(jnp.concatenate(parts, 0).astype(BF16), picks[m])
            found = part if found is None else found + part
        o_ref[:, k * WIDE : (k + 1) * WIDE] = dot(back, found.astype(BF16)).astype(BF16)


def to_columns(slots, pieces, places, channels):
    return pl.pallas_call(
        functools.partial(to_columns_kernel, places),
        out_shape=jax.ShapeDtypeStruct((channels * KXY, 2 * KZ * KXY), BF16),
        scratch_shapes=[pltpu.VMEM((WIDE, KXY * KXY), F32)],
        compiler_params=pltpu.CompilerParams(vmem_limit_bytes=SMALL),
        name="to_columns",
    )(slots, *pieces)


def fetch_lanes(hbm_ref, w_ref, sems, k):
    lanes = pl.ds(k * LANES, LANES)
    return pltpu.make_async_copy(hbm_ref.at[:, :, :, lanes], w_ref.at[:, :, :, lanes], sems.at[k])


def fetch_ahead(w_hbm, w_ref, sems, k):
    chunks = w_ref.shape[-1] // LANES

    @pl.when(k + AHEAD < chunks)
    def _():
        fetch_lanes(w_hbm, w_ref, sems, k + AHEAD).start()

    fetch_lanes(w_hbm, w_ref, sems, k).wait()


def mix_kernel(groups, a_ref, b_ref, c_ref, d_ref, w_hbm, e_ref, o_ref, s_ref, w_ref, sems):
    channels, outs, length = w_ref.shape[1:]
    for k in range(min(AHEAD, length // LANES)):
        fetch_lanes(w_hbm, w_ref, sems, k).start()
    own = outs // groups
    mask = depth_mask(LANES)
    per = SLOTS * KZ // LANES
    rows = a_ref.shape[1]
    s_ref[:rows] = (a_ref[0].astype(F32) + b_ref[0].astype(F32)).astype(BF16)
    s_ref[rows:] = (c_ref[0].astype(F32) + d_ref[0].astype(F32)).astype(BF16)

    def body(k, carry):
        slot = pl.multiple_of(k // per * SLOTS, SLOTS)
        part = pl.multiple_of(k % per * LANES, LANES)
        lane = pl.multiple_of(k * LANES, LANES)
        fetch_ahead(w_hbm, w_ref, sems, k)
        u = spread(s_ref[:, pl.ds(slot, SLOTS)], e_ref[:, pl.ds(part, LANES)], mask, channels)
        real = jnp.zeros((outs, LANES), F32)
        imag = jnp.zeros((outs, LANES), F32)
        for c in range(channels):
            w0 = w_ref[0, c, :, pl.ds(lane, LANES)].astype(F32)
            w1 = w_ref[1, c, :, pl.ds(lane, LANES)].astype(F32)
            ur, ui = u[0, c : c + 1], u[1, c : c + 1]
            real += w0 * ur - w1 * ui
            imag += w1 * ur + w0 * ui
        for g in range(groups):
            o_ref[g, 0, :, pl.ds(lane, LANES)] = real[g * own : (g + 1) * own].astype(BF16)
            o_ref[g, 1, :, pl.ds(lane, LANES)] = imag[g * own : (g + 1) * own].astype(BF16)
        return carry

    lax.fori_loop(0, length // LANES, body, 0)


def mix(sums, weights, table, groups):
    _, channels, outs, length = weights.shape
    return pl.pallas_call(
        functools.partial(mix_kernel, groups),
        out_shape=jax.ShapeDtypeStruct((groups, 2, outs // groups, length), BF16),
        in_specs=[resident()] * 4 + [anywhere(), resident()],
        scratch_shapes=[
            pltpu.VMEM((2 * sums[0].shape[1], sums[0].shape[2]), BF16),
            pltpu.VMEM(weights.shape, BF16),
            pltpu.SemaphoreType.DMA((length // LANES,)),
        ],
        compiler_params=pltpu.CompilerParams(vmem_limit_bytes=SMALL),
        cost_estimate=pl.CostEstimate(
            flops=4 * weights.size, bytes_accessed=2 * weights.size, transcendentals=0
        ),
        name="mix",
    )(*sums, weights, table)


def compress_kernel(a_ref, b_ref, et_ref, o_ref):
    width = SLOTS * KZ
    mask = depth_mask(width)
    lane = lax.broadcasted_iota(jnp.int32, (1, 1, width), 2)
    twice = jnp.where(lane % KZ == 0, 1.0, 2.0).astype(F32)
    for k in range(a_ref.shape[-1] // width):
        lanes = slice(k * width, (k + 1) * width)
        total = a_ref[:, :, lanes].astype(F32) + b_ref[:, :, lanes].astype(F32)
        out = gather_depth(total * twice, et_ref[...], mask)
        o_ref[:, k * SLOTS : (k + 1) * SLOTS] = out.astype(BF16)


def compress(kept, got, table_t):
    _, channels, length = kept.shape
    return pl.pallas_call(
        compress_kernel,
        out_shape=jax.ShapeDtypeStruct((2 * KZ * channels, length // KZ), BF16),
        compiler_params=pltpu.CompilerParams(vmem_limit_bytes=SMALL),
        name="compress",
    )(kept, got, table_t)


def unmix_kernel(s_ref, w_hbm, e_ref, et_ref, o_ref, adj_ref, w_ref, sems):
    channels, outs, length = w_ref.shape[1:]
    for k in range(min(AHEAD, length // LANES)):
        fetch_lanes(w_hbm, w_ref, sems, k).start()
    groups = s_ref.shape[0]
    mask = depth_mask(LANES)
    per = SLOTS * KZ // LANES
    wide = depth_mask(SLOTS * KZ)

    def chunk(k, carry):
        def body(j, inner):
            slot = pl.multiple_of(k * SLOTS, SLOTS)
            part = pl.multiple_of(j * LANES, LANES)
            lane = pl.multiple_of(k * SLOTS * KZ + j * LANES, LANES)
            fetch_ahead(w_hbm, w_ref, sems, k * per + j)
            table = e_ref[:, pl.ds(part, LANES)]
            pieces = [spread(s_ref[g, :, pl.ds(slot, SLOTS)], table, mask, outs // groups) for g in range(groups)]
            gr = jnp.concatenate([piece[0] for piece in pieces], 0)
            gi = jnp.concatenate([piece[1] for piece in pieces], 0)
            for c in range(channels):
                w0 = w_ref[0, c, :, pl.ds(lane, LANES)].astype(F32)
                w1 = w_ref[1, c, :, pl.ds(lane, LANES)].astype(F32)
                adj_ref[0, c : c + 1, pl.ds(part, LANES)] = jnp.sum(w0 * gr + w1 * gi, axis=0, keepdims=True)
                adj_ref[1, c : c + 1, pl.ds(part, LANES)] = jnp.sum(w0 * gi - w1 * gr, axis=0, keepdims=True)
            return inner

        lax.fori_loop(0, per, body, 0)
        out = gather_depth(adj_ref[...], et_ref[...], wide)
        o_ref[:, pl.ds(pl.multiple_of(k * SLOTS, SLOTS), SLOTS)] = out.astype(BF16)
        return carry

    lax.fori_loop(0, length // (SLOTS * KZ), chunk, 0)


def unmix(sums, weights, table, table_t):
    _, channels, outs, length = weights.shape
    return pl.pallas_call(
        unmix_kernel,
        out_shape=jax.ShapeDtypeStruct((2 * KZ * channels, length // KZ), BF16),
        in_specs=[resident(), anywhere(), resident(), resident()],
        scratch_shapes=[
            pltpu.VMEM((2, channels, SLOTS * KZ), F32),
            pltpu.VMEM(weights.shape, BF16),
            pltpu.SemaphoreType.DMA((length // LANES,)),
        ],
        compiler_params=pltpu.CompilerParams(vmem_limit_bytes=SMALL),
        cost_estimate=pl.CostEstimate(
            flops=4 * weights.size, bytes_accessed=2 * weights.size, transcendentals=0
        ),
        name="unmix",
    )(sums, weights, table, table_t)


def bits_of(count):
    return tuple(1 << k for k in reversed(range(count.bit_length() - 1)))


def offsets(route):
    found = [0]
    for bit in route:
        found = found + [k ^ bit for k in found]
    return found


def exchange(value, axis, offset):
    size = lax.axis_size(axis)
    return lax.ppermute(value, axis, [(k, k ^ offset) for k in range(size)])


def per_device(field, forcing, slot_column, w_spec, skip_gain, bias):
    channels, planes, grid_len, _ = field.shape
    slabs, capacity = slot_column.shape
    groups = lax.axis_size("chan")
    own_rows = forcing.shape[1]
    factor = float(grid_len) ** -1.5

    row_np, col_np = plane_tables(grid_len)
    depth_np = depth_tables(planes, grid_len)
    rt = jnp.asarray(half_width(row_np))
    bd = jnp.asarray(half_width(np.swapaxes(row_np, 1, 2)) * ml_dtypes.bfloat16(factor))
    tx = jnp.asarray(half_width(col_np))
    txt = jnp.asarray(half_width(col_np.T))
    tz = jnp.asarray(half_width(depth_np))
    ts = jnp.asarray(half_width(np.swapaxes(depth_np, 1, 2)))
    table = jnp.asarray(half_width(spread_table()))
    table_t = jnp.asarray(half_width(spread_table().T))
    first = np.arange(slabs)[:, None] * planes * np.arange(KZ)[None, :] % grid_len
    first = np.repeat(first * (2.0 * math.pi / grid_len), KXY, axis=1)
    phases = jnp.asarray(np.stack([np.cos(first), np.sin(first)], 1).astype(np.float32))
    phase = lax.dynamic_index_in_dim(phases, lax.axis_index("slab"), 0, keepdims=False)

    slots = slot_column[:, None, :]
    me_slab, me_chan = lax.axis_index("slab"), lax.axis_index("chan")
    slab_bits = bits_of(slabs)
    routes = (slab_bits, slab_bits[-1:] + slab_bits[:-1])
    orders = [offsets(route) for route in routes]
    places = tuple(orders[1].index(offset) for offset in orders[0])
    gathered_slots = jnp.take(slots, me_slab ^ np.array(orders[0]), axis=0)

    forced_parts = [forcing]
    for bit in bits_of(groups):
        forced_parts += [exchange(part, "chan", bit) for part in forced_parts]
    forced_places = (me_chan ^ np.array(offsets(bits_of(groups)))).astype(jnp.int32)

    def send_sums(coefs, others, after):
        parts = to_slots(gathered_slots, coefs, others, places, after)
        kept, sent = [parts[0], parts[2]], [parts[1], parts[3]]
        for step in reversed(range(len(slab_bits))):
            got = [exchange(part, "slab", route[step]) for part, route in zip(sent, routes)]
            if step == 0:
                return kept[0], got[0], kept[1], got[1]
            sums = [(mine.astype(F32) + other.astype(F32)).astype(BF16) for mine, other in zip(kept, got)]
            kept, sent = zip(*[jnp.split(part, 2, axis=0) for part in sums])

    def spread_spectra(own):
        pieces = [piece[None] for piece in jnp.split(own, 2, axis=0)]
        for step in range(len(slab_bits)):
            got = [exchange(piece, "slab", route[step]) for piece, route in zip(pieces, routes)]
            if step < len(slab_bits) - 1:
                pieces = [jnp.concatenate(pair, 0) for pair in zip(pieces, got)]
        return to_columns(gathered_slots, [pieces[0], got[0], pieces[1], got[1]], places, channels)

    tx_own = lax.dynamic_slice_in_dim(tx, lax.axis_index("chan") * own_rows, own_rows, 1)
    forced = analyse_forced(forcing, rt, tx_own, tz, phase, factor)
    others = [exchange(forced, "chan", k) for k in range(1, groups)]
    coefs = analyse(field, rt, tx, tz, phase, factor)
    partial = mix(send_sums(coefs, [forced] + others, forced_parts[1:2]), w_spec, table, groups)
    for bit in reversed(bits_of(groups)):
        pairs = partial.reshape((partial.shape[0] // 2, 2) + partial.shape[1:])
        side = (me_chan // bit) % 2
        mine = lax.dynamic_index_in_dim(pairs, side, 1, keepdims=False)
        got = exchange(lax.dynamic_index_in_dim(pairs, 1 - side, 1, keepdims=False), "chan", bit)
        if mine.shape[0] > 1:
            partial = (mine.astype(F32) + got.astype(F32)).astype(BF16)
    spectra = spread_spectra(compress(mine[0], got[0], table_t))

    gain_rows = jnp.repeat(skip_gain, KXY)[:, None]
    centre = np.zeros((KXY, 2, ZB, KXY), np.float32)
    centre[KXY // 2, 0, :, KXY // 2] = 1.0 / factor
    centre = jnp.asarray(np.tile(centre.reshape(KXY, 2 * HALF), (channels, 1)))
    shift = centre * jnp.repeat(bias / skip_gain, KXY)[:, None]
    coefs_gelu = jnp.stack(
        [skip_gain**3 * (C1 * C2), skip_gain * C1, skip_gain * 0.5, skip_gain**2 * (6.0 * C1 * C2)], 1
    )
    output, grads, back = middle(
        spectra, field, forced_parts, forced_places, coefs_gelu, 1.0 / gain_rows, shift, rt, bd, tx, txt, tz, ts, phase, 0.5 * factor
    )
    doubling = jnp.where(jnp.arange(KZ) == 0, 1.0, 2.0).astype(F32)
    doubling = jnp.tile(jnp.repeat(doubling, channels), 2)[:, None]
    parts = [part[0].astype(F32) for part in send_sums(back, [], [])]
    sums = jnp.concatenate([parts[0] + parts[1], parts[2] + parts[3]], 0)
    sums = (sums * doubling).astype(BF16)
    everyone = lax.all_gather(sums, "chan", axis=0)
    adjoint = spread_spectra(unmix(everyone, w_spec, table, table_t))
    gradient = finish(adjoint, grads, skip_gain * 0.5, bd, txt, ts, phase)
    return output, gradient


def solution(mesh):
    placed = (
        P("chan", "slab", None, None),
        P("slab", "chan", None),
        P(),
        P(None, "chan", None, "slab"),
        P("chan"),
        P("chan"),
    )
    return jax.shard_map(
        per_device,
        mesh=mesh,
        in_specs=placed,
        out_specs=(P("chan", "slab", None, None), P("chan", "slab", None, None)),
        check_vma=False,
    )
```
